256 devices in a mesh: space: 64 (over y, x, z_hi), rep: 4 (over z_lo, core).
Axes of the slice: x: 4, y: 4, z: 8 (z_hi: 4, z_lo: 2; z = z_hi * 2 + z_lo), core: 2. Of those that a mesh axis runs over, the one named last changes fastest.
Arguments:
- leaf_density: bfloat16 [888, 65536], P(None, 'space'), may hold values from -6 to 6
- upward_ops: bfloat16 [8, 888, 888], P(None, 'rep'), may hold values from -0.0625 to 0.0625
- far_ops: bfloat16 [12, 888, 888], P('rep'), may hold values from -0.0625 to 0.0625
- downward_ops: bfloat16 [8, 888, 888], P(None, 'rep'), may hold values from -0.1875 to 0.1875
- fine_lists: int32 [12, 65536], P('rep', 'space'), may hold values from 0 to 3071
- coarse_lists: int32 [12, 8192], P('rep', 'space'), may hold values from 0 to 383
Outputs:
- local_check: bfloat16 [888, 65536], P('rep', 'space')
The draws below stay inside these ranges and needn't reach their ends.
Inputs may be any that keep to these rules, and one draw needn't show every extreme that they name: `fine_lists`: entry k of box g names a box of the previous subtree (below 1024), of its own (below 2048) or of the next one; indices outside the grid of subtrees read zeros. `coarse_lists`: entry k of coarse box p names a coarse box of the previous coarse subtree (below 128), of its own (below 256) or of the next one; indices outside the grid read zeros.
All inputs are finite; a program needn't handle non-finite values.
Results may differ from the reference program's by a relative error of at most 0.013.
Values may be sent and summed in bfloat16 or wider, within the bound.
No kernel may reach another device: no remote copies, remote signals or barrier semaphores. Data moves between devices by JAX's collectives and lax.ppermute only.
A program may use at most 128 MiB of HBM per device.

```python
import jax
import jax.numpy as jnp

DENS = 888
SLOTS = 12
BOX_DEV = 1024
FINE = 65536
COARSE = 8192


def place_ends(entries, own_key, least, high):
    longest = entries.shape.index(max(entries.shape))
    spots = []
    for shift in (0, 1):
        where = [jax.random.randint(jax.random.fold_in(own_key, axis), (), 0, length) for axis, length in enumerate(entries.shape)]
        where[longest] = (where[longest] + shift) % entries.shape[longest]
        spots.append(tuple(where))
    return entries.at[spots[0]].set(least).at[spots[1]].set(high)


def levels(stream_key, extent, pieces, smallest, high):
    factor_of, own = 1.0, jax.random.fold_in(stream_key, 6)
    for position, shards_of in pieces:
        draws = jnp.exp(jax.random.uniform(jax.random.fold_in(own, position), (shards_of,), jnp.float32, smallest / len(pieces), high / len(pieces)))
        factor_of = factor_of * jnp.repeat(draws, extent[position] // shards_of).reshape([-1 if axis == position else 1 for axis in range(len(extent))])
    return factor_of


def bell_draw(own_key, dims, width, limit, pieces=(), held_as=jnp.bfloat16):
    drawn = jax.random.normal(own_key, dims, jnp.float32) * width
    if len(pieces) > 0:
        drawn = levels(own_key, dims, pieces, -0.22, 0.18) * drawn
    return jnp.clip(drawn, min=-limit, max=limit).astype(held_as)


def setup_inputs(seed: int = 0) -> dict:
    streams_of = jax.random.split(jax.random.key(seed), 7)
    return {
        "leaf_density": bell_draw(streams_of[0], (DENS, FINE), 1.0, 6.0, ((1, 64),)),
        "upward_ops": bell_draw(streams_of[1], (8, DENS, DENS), (8 * DENS) ** -0.5, 0.0625, ((1, 4),)),
        "far_ops": bell_draw(streams_of[2], (SLOTS, DENS, DENS), (SLOTS * DENS) ** -0.5, 0.0625, ((0, 4),)),
        "downward_ops": bell_draw(streams_of[3], (8, DENS, DENS), DENS ** -0.5, 0.1875, ((1, 4),)),
        "fine_lists": place_ends(jax.random.randint(streams_of[4], (SLOTS, FINE), 0, 3 * BOX_DEV), jax.random.fold_in(streams_of[4], 1), 0, (3 * BOX_DEV) - 1).astype(jnp.int32),
        "coarse_lists": place_ends(jax.random.randint(streams_of[5], (SLOTS, COARSE), 0, 3 * (BOX_DEV // 8)), jax.random.fold_in(streams_of[5], 1), 0, (3 * (BOX_DEV // 8)) - 1).astype(jnp.int32),
    }


coarse_scale = 0.5


def reference(leaf_density, upward_ops, far_ops, downward_ops, fine_lists, coarse_lists):
    density_rows = leaf_density.shape[0]
    fine_total = leaf_density.shape[1]
    coarse_total = fine_total // 8
    coarse_block = BOX_DEV // 8
    children = leaf_density.reshape(density_rows, coarse_total, 8).astype(jnp.float32)
    parents = jnp.einsum("crq,qpc->rp", upward_ops.astype(jnp.float32), children)
    coarse_up = parents.astype(jnp.bfloat16)
    padded = jnp.pad(leaf_density, ((0, 0), (BOX_DEV, BOX_DEV)))
    padded_up = jnp.pad(coarse_up, ((0, 0), (coarse_block, coarse_block)))
    anchor = (jnp.arange(fine_total, dtype=jnp.int32) // BOX_DEV) * BOX_DEV
    coarse_anchor = (jnp.arange(coarse_total, dtype=jnp.int32) // coarse_block) * coarse_block
    fine_check = jnp.zeros((density_rows, fine_total), jnp.float32)
    coarse_sum = jnp.zeros((density_rows, coarse_total), jnp.float32)
    for offset in range(SLOTS):
        sources = jnp.take(padded, (anchor + fine_lists[offset]).astype(jnp.int32), axis=1)
        fine_check = fine_check + jnp.dot(far_ops[offset], sources, preferred_element_type=jnp.float32)
        remote = jnp.take(padded_up, (coarse_anchor + coarse_lists[offset]).astype(jnp.int32), axis=1)
        coarse_sum = coarse_sum + jnp.dot(far_ops[offset], remote, preferred_element_type=jnp.float32)
    coarse_check = (coarse_scale * coarse_sum).astype(jnp.bfloat16)
    spread = jnp.einsum("crq,qp->rpc", downward_ops.astype(jnp.float32), coarse_check.astype(jnp.float32))
    return (fine_check + spread.reshape(density_rows, fine_total)).astype(jnp.bfloat16)
```

```python
import functools

import jax
import jax.numpy as jnp
from jax import lax
from jax.experimental import pallas as pl
from jax.experimental.pallas import tpu as pltpu
from jax.sharding import PartitionSpec as P

bf16, f32 = jnp.bfloat16, jnp.float32
both = ("space", "rep")
coarse_scale = 0.5
rows, wide, tiles = 888, 896, 7
boxes, half = 1024, 512
parents = 128
share = 222
chunks = 2
chunk = half // chunks
window = 6 * half
vmem = pltpu.CompilerParams(vmem_limit_bytes=56 << 20)


def one_hop(groups):
    up = [(4 * s + 2 + c, 4 * (s + 1) + c) for s in range(groups - 1) for c in (0, 1)]
    return up + [(j, i) for i, j in up]


def across(groups, flip):
    return [(4 * s + r, 4 * s + (r ^ flip)) for s in range(groups) for r in range(4)]


def call(kernel, scalars, args, in_specs, out_specs, out_shape, grid=(1,), scratch=(), cost=0):
    moved = sum(a.size * a.dtype.itemsize for a in args)
    return pl.pallas_call(
        kernel,
        grid_spec=pltpu.PrefetchScalarGridSpec(
            num_scalar_prefetch=1,
            grid=grid,
            in_specs=in_specs,
            out_specs=out_specs,
            scratch_shapes=scratch,
        ),
        out_shape=out_shape,
        compiler_params=vmem,
        cost_estimate=pl.CostEstimate(flops=cost, bytes_accessed=moved, transcendentals=0),
    )(scalars, *args)


def whole(a):
    zeros = (0,) * a.ndim
    return pl.BlockSpec(a.shape, lambda *_: zeros)


def turn_kernel(first, x_ref, o_ref):
    width = x_ref.shape[1]
    tall = jnp.concatenate([x_ref[...].astype(f32), jnp.zeros((wide - rows, width), f32)], 0)
    o_ref[...] = tall.T.astype(bf16)


def turned(x, first, count, width):
    return call(
        turn_kernel,
        first,
        (x,),
        [pl.BlockSpec((rows, width), lambda i, s: (0, s[0] + i))],
        pl.BlockSpec((width, wide), lambda i, s: (i, 0)),
        jax.ShapeDtypeStruct((count * width, wide), bf16),
        grid=(count,),
        cost=count * width * 4000000,
    )


def to_planes(src, dst, height):
    for s in range(tiles - 1):
        dst[pl.ds(s * height, height), :] = src[:, s * 128 : (s + 1) * 128].astype(f32)
    last = src[:, (tiles - 1) * 128 :].astype(f32)
    if last.shape[1] < 128:
        last = jnp.concatenate([last, jnp.zeros((height, 128 - last.shape[1]), f32)], 1)
    dst[pl.ds((tiles - 1) * height, height), :] = last


def every_eighth(planes, height, child, count):
    parts = [planes[pl.ds(s * height + child, count, stride=8), :] for s in range(tiles)]
    return jnp.concatenate(parts, 1).astype(bf16)


def up_kernel(sc, ops, other, *refs):
    mine, o_ref, op_planes, box_planes = refs[:-3], refs[-3], refs[-2], refs[-1]
    to_planes(ops, op_planes, 8 * share)
    for s in range(tiles):
        lanes = slice(s * 128, (s + 1) * 128)
        for i, part in enumerate(mine):
            at = pl.multiple_of(s * boxes + sc[0] * half + i * chunk, chunk)
            box_planes[pl.ds(at, chunk), :] = part[:, lanes].astype(f32)
        at = pl.multiple_of(s * boxes + (1 - sc[0]) * half, half)
        box_planes[pl.ds(at, half), :] = other[:, lanes].astype(f32)
    total = None
    for child in range(8):
        left = every_eighth(op_planes, 8 * share, child, share)
        right = every_eighth(box_planes, boxes, child, parents)
        term = lax.dot_general(left, right, (((1,), (1,)), ((), ())), preferred_element_type=f32)
        total = term if total is None else total + term
    o_ref[...] = total.astype(bf16)


def parent_rows(sc, ops, mine, other):
    args = (ops, other, *mine)
    return call(
        up_kernel,
        sc,
        args,
        [whole(a) for a in args],
        pl.BlockSpec((share, parents), lambda *_: (0, 0)),
        jax.ShapeDtypeStruct((share, parents), bf16),
        scratch=[
            pltpu.VMEM((tiles * 8 * share, 128), f32),
            pltpu.VMEM((tiles * boxes, 128), f32),
        ],
        cost=4000000000,
    )


def coarse_kernel(sc, lists, far, own, a, b, own_o, ab_o, send, keep, picked, result):
    c, l = sc[0], sc[1]
    wanted = lists[...]
    count = wanted.shape[1]
    near = jnp.where(l == 0, 0, 2 * parents)
    spot = lax.broadcasted_iota(jnp.int32, (parents, count), 0)
    hot = jnp.concatenate(
        [
            (spot == wanted - base).astype(f32).astype(bf16)
            for base in (parents, near, 2 * parents - near)
        ],
        0,
    )

    def pick(*parts):
        return jnp.dot(jnp.concatenate(parts, 1), hot, preferred_element_type=f32)

    lo, hi = slice(0, parents), slice(parents, 2 * parents)
    a_o, b_o = ab_o[:, : 2 * parents], ab_o[:, 2 * parents :]
    found = (
        (pick(own[:, lo], a[:, hi], b[:, lo]), pick(own[:, hi], a[:, lo], b[:, hi])),
        (pick(own_o[:, lo], a_o[:, hi], b_o[:, lo]), pick(own_o[:, hi], a_o[:, lo], b_o[:, hi])),
    )
    for j in range(4):
        x, y = j // 2, j % 2
        mine = jnp.where(l == x, found[0][0], found[0][1])
        theirs = jnp.where(l == x, found[1][0], found[1][1])
        picked[pl.ds(share * j, share), :] = jnp.where(c == y, mine, theirs)
    sources = picked[...].astype(bf16)
    total = None
    for k in range(3):
        term = jnp.dot(
            far[k], sources[:, k * parents : (k + 1) * parents], preferred_element_type=f32
        )
        total = term if total is None else total + term
    result[pl.ds(0, rows), :] = total * coarse_scale
    result[pl.ds(rows, wide - rows), :] = jnp.zeros((wide - rows, parents), f32)
    part = wide // 2
    keep[...] = result[pl.ds(pl.multiple_of(c * part, part), part), :]
    send[...] = result[pl.ds(pl.multiple_of((1 - c) * part, part), part), :].astype(bf16)


def coarse_partial(sc, lists, far, own, a, b, own_o, ab_o):
    args = (lists, far, own, a, b, own_o, ab_o)
    shape = (wide // 2, parents)
    spec = pl.BlockSpec(shape, lambda *_: (0, 0))
    return call(
        coarse_kernel,
        sc,
        args,
        [whole(x) for x in args],
        [spec, spec],
        [jax.ShapeDtypeStruct(shape, bf16), jax.ShapeDtypeStruct(shape, f32)],
        scratch=[pltpu.VMEM((rows, 3 * parents), f32), pltpu.VMEM((wide, parents), f32)],
        cost=3000000000,
    )


def down_kernel(sc, ops, mine, other, o_ref, op_planes, check, turned_rows):
    c, part = sc[0], wide // 2
    to_planes(ops, op_planes, 8 * share)
    check[pl.ds(pl.multiple_of(c * part, part), part), :] = mine[...]
    check[pl.ds(pl.multiple_of((1 - c) * part, part), part), :] = other[...]
    whole_check = check[...]
    for child in range(8):
        left = every_eighth(op_planes, 8 * share, child, share)
        z = jnp.dot(left, whole_check, preferred_element_type=f32)
        z = jnp.concatenate([z, jnp.zeros((256 - share, parents), f32)], 0).T
        for t in (0, 1):
            turned_rows[pl.ds(t * boxes + child, parents, stride=8), :] = z[
                :, t * 128 : (t + 1) * 128
            ]
    o_ref[pl.ds(0, 128), :] = turned_rows[pl.ds(0, boxes), :].T
    o_ref[pl.ds(128, share - 128), :] = turned_rows[pl.ds(boxes, boxes), :].T[: share - 128]


def downward(sc, ops, mine, other):
    args = (ops, mine, other)
    return call(
        down_kernel,
        sc,
        args,
        [whole(x) for x in args],
        pl.BlockSpec((share, boxes), lambda *_: (0, 0)),
        jax.ShapeDtypeStruct((share, boxes), f32),
        scratch=[
            pltpu.VMEM((tiles * 8 * share, 128), f32),
            pltpu.VMEM((wide, parents), bf16),
            pltpu.VMEM((2 * boxes, 128), f32),
        ],
        cost=3000000000,
    )


pitch, step_boxes, unroll = window + 8, 512, 32


def gather_kernel(spots, *refs):
    pieces, o_ref, planes, got = refs[:-3], refs[-3], refs[-2], refs[-1]
    step = pl.program_id(0)
    depth = step_boxes + 8

    @pl.when(step == 0)
    def _():
        at = 0
        for piece in pieces:
            count = piece.shape[0]
            for s in range(tiles):
                planes[pl.ds(s * pitch + at, count), :] = piece[
                    :, s * 128 : (s + 1) * 128
                ].astype(f32)
            at += count

    def body(i, carry):
        found = [
            planes[pl.ds(spots[step * step_boxes + i * unroll + u], 8, stride=pitch), :]
            for u in range(unroll)
        ]
        for u in range(unroll):
            got[pl.ds(i * unroll + u, 8, stride=depth), :] = found[u]
        return carry

    lax.fori_loop(0, step_boxes // unroll, body, 0)
    for s in range(tiles):
        o_ref[0, :, s * 128 : (s + 1) * 128] = got[pl.ds(s * depth, step_boxes), :].astype(bf16)


def gathered(spots, pieces):
    steps = boxes // step_boxes
    return call(
        gather_kernel,
        spots,
        tuple(pieces),
        [whole(p) for p in pieces],
        pl.BlockSpec((1, step_boxes, wide), lambda i, s: (i // steps, i % steps, 0)),
        jax.ShapeDtypeStruct((3, boxes, wide), bf16),
        grid=(3 * steps,),
        scratch=[
            pltpu.VMEM((8 * pitch, 128), f32),
            pltpu.VMEM((8 * (step_boxes + 8), 128), f32),
        ],
        cost=8000000000,
    )


def far_kernel(sc, far, sources, send, keep, result):
    c = sc[0]
    total = None
    for k in range(3):
        term = lax.dot_general(
            far[k], sources[k][:, :rows], (((1,), (1,)), ((), ())), preferred_element_type=f32
        )
        total = term if total is None else total + term
    result[...] = total
    for x in (0, 1):
        first = result[pl.ds(share * 2 * x, share), :]
        second = result[pl.ds(share * (2 * x + 1), share), :]
        keep[x] = jnp.where(c == 0, first, second)
        send[x] = jnp.where(c == 0, second, first).astype(bf16)


def far_partial(sc, far, sources, start, count, width=256):
    shape = (2, share, count)
    spec = pl.BlockSpec((2, share, width), lambda i, s: (0, 0, i))
    skip = start // width
    return call(
        far_kernel,
        sc,
        (far, sources),
        [whole(far), pl.BlockSpec((3, width, wide), lambda i, s: (0, skip + i, 0))],
        [spec, spec],
        [jax.ShapeDtypeStruct(shape, bf16), jax.ShapeDtypeStruct(shape, f32)],
        grid=(count // width,),
        scratch=[pltpu.VMEM((rows, width), f32)],
        cost=3 * 2 * rows * rows * count,
    )


def local(leaf_density, upward_ops, far_ops, downward_ops, fine_lists, coarse_lists):
    groups = lax.axis_size("space")
    rep = lax.axis_index("rep")
    l, c = rep // 2, rep % 2
    sc = jnp.stack([c, l]).astype(jnp.int32)
    hop = functools.partial(lax.ppermute, axis_name=both, perm=one_hop(groups))
    zswap = functools.partial(lax.ppermute, axis_name=both, perm=across(groups, 2))
    cswap = functools.partial(lax.ppermute, axis_name=both, perm=across(groups, 1))

    def at(i):
        return jnp.reshape(i, (1,)).astype(jnp.int32)

    mine = [turned(leaf_density, at(c * chunks + i), 1, chunk) for i in range(chunks)]
    other = turned(leaf_density, at((1 - c) * 2), 2, 256)
    a = [hop(m) for m in mine]
    b = [zswap(x) for x in a]
    a_o = [cswap(x) for x in a]
    b_o = [cswap(x) for x in b]

    up_ops = jnp.transpose(upward_ops, (1, 0, 2)).reshape(8 * share, rows)
    down_ops = jnp.transpose(downward_ops, (1, 0, 2)).reshape(8 * share, rows)
    up = parent_rows(sc, up_ops, mine, other)
    own = jnp.concatenate([up, zswap(up)], 1)
    ca = hop(own)
    cb = zswap(ca)
    own_o = cswap(own)
    cab_o = cswap(jnp.concatenate([ca, cb], 1))
    send, keep = coarse_partial(
        sc, coarse_lists.reshape(1, 3 * parents), far_ops, own, ca, cb, own_o, cab_o
    )
    part = keep + cswap(send).astype(f32)
    check = (part + zswap(part.astype(bf16)).astype(f32)).astype(bf16)
    spread = downward(sc, down_ops, check, cswap(check))

    which, side, offset = fine_lists >> 10, (fine_lists >> 9) & 1, fine_lists & (half - 1)
    base = jnp.where(which == 1, 0, jnp.where((which == 0) == (l == 0), 2, 4))
    spots = (base + jnp.where(side == c, 0, 1)) * half + offset
    picked = gathered(spots.reshape(-1), [*mine, other, *a, *a_o, *b, *b_o])

    outs = []
    for start in (0, half):
        send, keep = far_partial(sc, far_ops, picked, start, half)
        part = keep + cswap(send).astype(f32)
        away = lax.dynamic_index_in_dim(part, 1 - l, 0, keepdims=False).astype(bf16)
        here = lax.dynamic_index_in_dim(part, l, 0, keepdims=False)
        outs.append(
            here + zswap(away).astype(f32) + lax.slice_in_dim(spread, start, start + half, axis=1)
        )
    return jnp.concatenate(outs, 1).astype(bf16)


def solution(mesh):
    return jax.shard_map(
        local,
        mesh=mesh,
        in_specs=(
            P(None, "space"),
            P(None, "rep", None),
            P("rep", None, None),
            P(None, "rep", None),
            P("rep", "space"),
            P("rep", "space"),
        ),
        out_specs=P("rep", "space"),
        check_vma=False,
    )
```

```python
import functools

import jax
import jax.numpy as jnp
from jax import lax
from jax.experimental import pallas as pl
from jax.experimental.pallas import tpu as pltpu
from jax.sharding import PartitionSpec as P

bf16, f32 = jnp.bfloat16, jnp.float32
both = ("space", "rep")
coarse_scale = 0.5
rows, wide, tiles = 888, 896, 7
boxes, half = 1024, 512
parents = 128
share = 222
chunks = 2
chunk = half // chunks
early = 6 * half - 2 * chunk
vmem = pltpu.CompilerParams(vmem_limit_bytes=24 << 20)


def one_hop(groups):
    up = [(4 * s + 2 + c, 4 * ((s + 1) % groups) + c) for s in range(groups) for c in (0, 1)]
    return up + [(j, i) for i, j in up]


def across(groups, flip):
    return [(4 * s + r, 4 * s + (r ^ flip)) for s in range(groups) for r in range(4)]


def call(kernel, scalars, args, in_specs, out_specs, out_shape, grid=(1,), scratch=()):
    return pl.pallas_call(
        kernel,
        grid_spec=pltpu.PrefetchScalarGridSpec(
            num_scalar_prefetch=1,
            grid=grid,
            in_specs=in_specs,
            out_specs=out_specs,
            scratch_shapes=scratch,
        ),
        out_shape=out_shape,
        compiler_params=vmem,
        cost_estimate=pl.CostEstimate(flops=0, bytes_accessed=0, transcendentals=0),
    )(scalars, *args)


def whole(a):
    return pl.BlockSpec(memory_space=pltpu.VMEM)


def turn_kernel(first, x_ref, o_ref):
    width = x_ref.shape[1]
    tall = jnp.concatenate([x_ref[...].astype(f32), jnp.zeros((wide - rows, width), f32)], 0)
    o_ref[...] = tall.T.astype(bf16)


def turned(x, first, count, width):
    return call(
        turn_kernel,
        first,
        (x,),
        [pl.BlockSpec((rows, width), lambda i, s: (0, s[0] + i))],
        pl.BlockSpec((width, wide), lambda i, s: (i, 0)),
        jax.ShapeDtypeStruct((count * width, wide), bf16),
        grid=(count,),
    )


def to_planes(src, dst, height):
    for s in range(tiles - 1):
        dst[pl.ds(s * height, height), :] = src[:, s * 128 : (s + 1) * 128].astype(f32)
    last = src[:, (tiles - 1) * 128 :].astype(f32)
    if last.shape[1] < 128:
        last = jnp.concatenate([last, jnp.zeros((height, 128 - last.shape[1]), f32)], 1)
    dst[pl.ds((tiles - 1) * height, height), :] = last


def every_eighth(planes, height, child, count):
    parts = [planes[pl.ds(s * height + child, count, stride=8), :] for s in range(tiles)]
    return jnp.concatenate(parts, 1).astype(bf16)


def up_kernel(sc, ops, other, *refs):
    mine, o_ref, op_planes, box_planes = refs[:-3], refs[-3], refs[-2], refs[-1]
    to_planes(ops, op_planes, 8 * share)
    for s in range(tiles):
        lanes = slice(s * 128, (s + 1) * 128)
        for i, part in enumerate(mine):
            at = pl.multiple_of(s * boxes + sc[0] * half + i * chunk, chunk)
            box_planes[pl.ds(at, chunk), :] = part[:, lanes].astype(f32)
        at = pl.multiple_of(s * boxes + (1 - sc[0]) * half, half)
        box_planes[pl.ds(at, half), :] = other[:, lanes].astype(f32)
    total = None
    for child in range(8):
        left = every_eighth(op_planes, 8 * share, child, share)
        right = every_eighth(box_planes, boxes, child, parents)
        term = lax.dot_general(left, right, (((1,), (1,)), ((), ())), preferred_element_type=f32)
        total = term if total is None else total + term
    o_ref[...] = total.astype(bf16)


def parent_rows(sc, ops, mine, other):
    args = (ops, other, *mine)
    return call(
        up_kernel,
        sc,
        args,
        [whole(a) for a in args],
        pl.BlockSpec((share, parents), lambda *_: (0, 0)),
        jax.ShapeDtypeStruct((share, parents), bf16),
        scratch=[
            pltpu.VMEM((tiles * 8 * share, 128), f32),
            pltpu.VMEM((tiles * boxes, 128), f32),
        ],
    )


def coarse_kernel(sc, lists, far, own, a, b, own_o, ab_o, send, keep, picked, result):
    c, l = sc[0], sc[1]
    wanted = lists[...]
    count = wanted.shape[1]
    spot = lax.broadcasted_iota(jnp.int32, (parents, count), 0)
    hot = jnp.concatenate(
        [
            (spot == wanted - base).astype(f32).astype(bf16)
            for base in (parents, sc[2], sc[3])
        ],
        0,
    )

    def pick(*parts):
        return jnp.dot(jnp.concatenate(parts, 1), hot, preferred_element_type=f32)

    lo, hi = slice(0, parents), slice(parents, 2 * parents)
    a_o, b_o = ab_o[:, : 2 * parents], ab_o[:, 2 * parents :]
    found = (
        (pick(own[:, lo], a[:, hi], b[:, lo]), pick(own[:, hi], a[:, lo], b[:, hi])),
        (pick(own_o[:, lo], a_o[:, hi], b_o[:, lo]), pick(own_o[:, hi], a_o[:, lo], b_o[:, hi])),
    )
    for j in range(4):
        x, y = j // 2, j % 2
        mine = jnp.where(l == x, found[0][0], found[0][1])
        theirs = jnp.where(l == x, found[1][0], found[1][1])
        picked[pl.ds(share * j, share), :] = jnp.where(c == y, mine, theirs)
    sources = picked[...].astype(bf16)
    total = None
    for k in range(3):
        term = jnp.dot(
            far[k], sources[:, k * parents : (k + 1) * parents], preferred_element_type=f32
        )
        total = term if total is None else total + term
    result[pl.ds(0, rows), :] = total * coarse_scale
    result[pl.ds(rows, wide - rows), :] = jnp.zeros((wide - rows, parents), f32)
    part = wide // 2
    keep[...] = result[pl.ds(pl.multiple_of(c * part, part), part), :]
    send[...] = result[pl.ds(pl.multiple_of((1 - c) * part, part), part), :].astype(bf16)


def coarse_partial(sc, lists, far, own, a, b, own_o, ab_o):
    args = (lists, far, own, a, b, own_o, ab_o)
    shape = (wide // 2, parents)
    spec = pl.BlockSpec(shape, lambda *_: (0, 0))
    return call(
        coarse_kernel,
        sc,
        args,
        [whole(x) for x in args],
        [spec, spec],
        [jax.ShapeDtypeStruct(shape, bf16), jax.ShapeDtypeStruct(shape, f32)],
        scratch=[pltpu.VMEM((rows, 3 * parents), f32), pltpu.VMEM((wide, parents), f32)],
    )


def down_kernel(sc, ops, mine, other, o_ref, op_planes, check, turned_rows):
    c, part = sc[0], wide // 2
    to_planes(ops, op_planes, 8 * share)
    check[pl.ds(pl.multiple_of(c * part, part), part), :] = mine[...]
    check[pl.ds(pl.multiple_of((1 - c) * part, part), part), :] = other[...]
    whole_check = check[...]
    for child in range(8):
        left = every_eighth(op_planes, 8 * share, child, share)
        z = jnp.dot(left, whole_check, preferred_element_type=f32)
        z = jnp.concatenate([z, jnp.zeros((256 - share, parents), f32)], 0).T
        for t in (0, 1):
            turned_rows[pl.ds(t * boxes + child, parents, stride=8), :] = z[
                :, t * 128 : (t + 1) * 128
            ]
    o_ref[pl.ds(0, 128), :] = turned_rows[pl.ds(0, boxes), :].T
    o_ref[pl.ds(128, share - 128), :] = turned_rows[pl.ds(boxes, boxes), :].T[: share - 128]


def downward(sc, ops, mine, other):
    args = (ops, mine, other)
    return call(
        down_kernel,
        sc,
        args,
        [whole(x) for x in args],
        pl.BlockSpec((share, boxes), lambda *_: (0, 0)),
        jax.ShapeDtypeStruct((share, boxes), f32),
        scratch=[
            pltpu.VMEM((tiles * 8 * share, 128), f32),
            pltpu.VMEM((wide, parents), bf16),
            pltpu.VMEM((2 * boxes, 128), f32),
        ],
    )


pitch, step_boxes, unroll = early + 8, 512, 32


def gather_kernel(spots, *refs):
    pieces, o_ref, planes, got = refs[:-3], refs[-3], refs[-2], refs[-1]
    step = pl.program_id(0)
    depth = step_boxes + 8

    @pl.when(step == 0)
    def _():
        at = 0
        for piece in pieces:
            count = piece.shape[0]
            for s in range(tiles):
                planes[pl.ds(s * pitch + at, count), :] = piece[
                    :, s * 128 : (s + 1) * 128
                ].astype(f32)
            at += count
        for s in range(tiles):
            planes[pl.ds(s * pitch + early, 8), :] = jnp.zeros((8, 128), f32)

    def body(i, carry):
        found = [
            planes[pl.ds(spots[step * step_boxes + i * unroll + u], 8, stride=pitch), :]
            for u in range(unroll)
        ]
        for u in range(unroll):
            got[pl.ds(i * unroll + u, 8, stride=depth), :] = found[u]
        return carry

    lax.fori_loop(0, step_boxes // unroll, body, 0)
    for s in range(tiles):
        o_ref[0, :, s * 128 : (s + 1) * 128] = got[pl.ds(s * depth, step_boxes), :].astype(bf16)


def gathered(spots, pieces):
    steps = boxes // step_boxes
    return call(
        gather_kernel,
        spots,
        tuple(pieces),
        [whole(p) for p in pieces],
        pl.BlockSpec((1, step_boxes, wide), lambda i, s: (i // steps, i % steps, 0)),
        jax.ShapeDtypeStruct((3, boxes, wide), bf16),
        grid=(3 * steps,),
        scratch=[
            pltpu.VMEM((8 * pitch, 128), f32),
            pltpu.VMEM((8 * (step_boxes + 8), 128), f32),
        ],
    )


def far_kernel(sc, far, sources, lists, late, late_o, send, keep, result):
    c = sc[0]
    width = sources.shape[1]
    spot = lax.broadcasted_iota(jnp.int32, (width, 128), 1).astype(f32)
    late_boxes = jnp.concatenate([late[...], late_o[...]], 0)
    total = None
    for k in range(3):
        wanted = jnp.broadcast_to(lists[k].astype(f32), (128, width)).T
        hot = jnp.concatenate(
            [
                (wanted == spot + float(base)).astype(f32).astype(bf16)
                for base in range(0, 2 * chunk, 128)
            ],
            1,
        )
        found = jnp.dot(hot, late_boxes, preferred_element_type=f32) + sources[k].astype(f32)
        term = lax.dot_general(
            far[k],
            found.astype(bf16)[:, :rows],
            (((1,), (1,)), ((), ())),
            preferred_element_type=f32,
        )
        total = term if total is None else total + term
    result[...] = total
    for x in (0, 1):
        first = result[pl.ds(share * 2 * x, share), :]
        second = result[pl.ds(share * (2 * x + 1), share), :]
        keep[x] = jnp.where(c == 0, first, second)
        send[x] = jnp.where(c == 0, second, first).astype(bf16)


def far_partial(sc, far, sources, lists, late, late_o, start, count, width=256):
    shape = (2, share, count)
    spec = pl.BlockSpec((2, share, width), lambda i, s: (0, 0, i))
    skip = start // width
    return call(
        far_kernel,
        sc,
        (far, sources, lists, late, late_o),
        [
            whole(far),
            pl.BlockSpec((3, width, wide), lambda i, s: (0, skip + i, 0)),
            pl.BlockSpec((3, 1, width), lambda i, s: (0, 0, skip + i)),
            whole(late),
            whole(late_o),
        ],
        [spec, spec],
        [jax.ShapeDtypeStruct(shape, bf16), jax.ShapeDtypeStruct(shape, f32)],
        grid=(count // width,),
        scratch=[pltpu.VMEM((rows, width), f32)],
    )


def after(x, *others):
    return lax.optimization_barrier((x, *others))[0]


def local(leaf_density, upward_ops, far_ops, downward_ops, fine_lists, coarse_lists):
    groups = lax.axis_size("space")
    group, rep = lax.axis_index("space"), lax.axis_index("rep")
    l, c = rep >> 1, rep & 1
    no_previous, no_next = group == 0, group == groups - 1
    nowhere = -16384
    base_previous = jnp.where(no_previous, nowhere, 0)
    base_next = jnp.where(no_next, nowhere, 2 * parents)
    sc = jnp.stack(
        [
            c,
            l,
            jnp.where(l == 0, base_previous, base_next),
            jnp.where(l == 0, base_next, base_previous),
        ]
    ).astype(jnp.int32)
    hop = functools.partial(lax.ppermute, axis_name=both, perm=one_hop(groups))
    zswap = functools.partial(lax.ppermute, axis_name=both, perm=across(groups, 2))
    cswap = functools.partial(lax.ppermute, axis_name=both, perm=across(groups, 1))

    def at(i):
        return jnp.reshape(i, (1,)).astype(jnp.int32)

    up_ops = jnp.transpose(upward_ops, (1, 0, 2)).reshape(8 * share, rows)
    down_ops = jnp.transpose(downward_ops, (1, 0, 2)).reshape(8 * share, rows)

    mine = [turned(leaf_density, at(c * chunks + i), 1, chunk) for i in range(chunks)]
    a = [hop(m) for m in mine]
    other = turned(leaf_density, at((1 - c) * 2), 2, 256)
    up = parent_rows(sc, up_ops, mine, other)
    first = after(a[0], up)
    b = [zswap(first)]
    a_o = [cswap(first)]
    own = jnp.concatenate([up, zswap(up)], 1)
    ca = hop(own)
    own_o = cswap(own)
    second = after(a[1], own)
    b.append(zswap(second))
    a_o.append(cswap(second))
    cb = zswap(ca)
    b_o = [cswap(x) for x in b]
    cab_o = cswap(jnp.concatenate([ca, cb], 1))

    which, side, offset = fine_lists >> 10, (fine_lists >> 9) & 1, fine_lists & (half - 1)
    outside = ((which == 0) & no_previous) | ((which == 2) & no_next)
    direct = (which == 0) == (l == 0)
    theirs = (side != c).astype(jnp.int32)
    is_late = (which != 1) & ~direct & (offset >= half - chunk)
    spots = jnp.where(
        which == 1,
        theirs * half + offset,
        jnp.where(
            direct,
            2 * half + theirs * half + offset,
            4 * half + theirs * (half - chunk) + offset,
        ),
    )
    spots = jnp.where(outside | is_late, early, spots)
    late_lists = jnp.where(is_late & ~outside, theirs * chunk + offset - (half - chunk), -1)
    late_lists = late_lists.reshape(3, 1, boxes)
    picked = gathered(spots.reshape(-1), [*mine, other, *a, *a_o, b[0], b_o[0]])

    def summed(send, keep):
        part = keep + cswap(send).astype(f32)
        away = lax.dynamic_index_in_dim(part, 1 - l, 0, keepdims=False).astype(bf16)
        here = lax.dynamic_index_in_dim(part, l, 0, keepdims=False)
        return here, zswap(away), away

    late = (b[1], b_o[1])
    send, keep = far_partial(sc, far_ops, picked, late_lists, *late, 0, half)
    left = summed(send, keep)
    send, keep = coarse_partial(
        after(sc, send), coarse_lists.reshape(1, 3 * parents), far_ops, own, ca, cb, own_o, cab_o
    )
    part = keep + cswap(send).astype(f32)
    send, keep = far_partial(after(sc, part, left[2]), far_ops, picked, late_lists, *late, half, half)
    right = summed(send, keep)
    check = (part + zswap(part.astype(bf16)).astype(f32)).astype(bf16)
    spread = downward(sc, down_ops, check, cswap(check))

    fine = jnp.concatenate([here + there.astype(f32) for here, there, _ in (left, right)], 1)
    return (fine + spread).astype(bf16)


def solution(mesh):
    return jax.shard_map(
        local,
        mesh=mesh,
        in_specs=(
            P(None, "space"),
            P(None, "rep", None),
            P("rep", None, None),
            P(None, "rep", None),
            P("rep", "space"),
            P("rep", "space"),
        ),
        out_specs=P("rep", "space"),
        check_vma=False,
    )
```

```python
import functools

import jax
import jax.numpy as jnp
from jax import lax
from jax.experimental import pallas as pl
from jax.experimental.pallas import tpu as pltpu
from jax.sharding import PartitionSpec as P

bf16, f32 = jnp.bfloat16, jnp.float32
both = ("space", "rep")
coarse_scale = 0.5
rows, wide, tiles = 888, 896, 7
boxes, half = 1024, 512
parents = 128
share = 222
chunks = 2
chunk = half // chunks
early = 6 * half - 2 * chunk


def one_hop(groups):
    up = [(4 * s + 2 + c, 4 * ((s + 1) % groups) + c) for s in range(groups) for c in (0, 1)]
    return up + [(j, i) for i, j in up]


def across(groups, flip):
    return [(4 * s + r, 4 * s + (r ^ flip)) for s in range(groups) for r in range(4)]


def call(kernel, scalars, args, in_specs, out_specs, out_shape, limit, grid=(1,), scratch=()):
    return pl.pallas_call(
        kernel,
        grid_spec=pltpu.PrefetchScalarGridSpec(
            num_scalar_prefetch=1,
            grid=grid,
            in_specs=in_specs,
            out_specs=out_specs,
            scratch_shapes=scratch,
        ),
        out_shape=out_shape,
        compiler_params=pltpu.CompilerParams(vmem_limit_bytes=limit << 20),
        cost_estimate=pl.CostEstimate(flops=0, bytes_accessed=0, transcendentals=0),
    )(scalars, *args)


def whole(a=None):
    return pl.BlockSpec(memory_space=pltpu.VMEM)


def turn_kernel(firsts, x_ref, *outs):
    for n, o_ref in enumerate(outs):
        for i in range(o_ref.shape[0] // 128):
            part = x_ref[:, pl.ds(pl.multiple_of(firsts[n] + i * 128, 128), 128)].astype(f32)
            tall = jnp.concatenate([part, jnp.zeros((wide - rows, 128), f32)], 0)
            o_ref[pl.ds(i * 128, 128), :] = tall.T.astype(bf16)


def turned(x, firsts, counts):
    shapes = [jax.ShapeDtypeStruct((n, wide), bf16) for n in counts]
    return call(turn_kernel, firsts, (x,), [whole()], [whole() for _ in counts], shapes, 8)


def small(kernel, sc, args, shapes, limit=6):
    shapes = [jax.ShapeDtypeStruct(*s) for s in shapes]
    return call(kernel, sc, args, [whole() for _ in args], [whole() for _ in shapes], shapes, limit)


def join_kernel(sc, *refs):
    at = 0
    for part in refs[:-1]:
        refs[-1][:, at : at + part.shape[1]] = part[...]
        at += part.shape[1]


def joined(sc, *parts):
    width = sum(p.shape[1] for p in parts)
    return small(join_kernel, sc, parts, [((parts[0].shape[0], width), bf16)])[0]


def split_kernel(sc, keep, got, here, away):
    l = sc[1]
    here[...] = keep[l] + got[l].astype(f32)
    away[...] = (keep[1 - l] + got[1 - l].astype(f32)).astype(bf16)


def add_kernel(sc, one, two, *outs):
    total = one[...] + two[...].astype(f32)
    for o_ref in outs:
        o_ref[...] = total.astype(o_ref.dtype)


def last_kernel(sc, spread, *refs):
    o_ref, at = refs[-1], 0
    for here, there in zip(refs[:-1:2], refs[1:-1:2]):
        lanes = slice(at, at + here.shape[1])
        o_ref[:, lanes] = (here[...] + there[...].astype(f32) + spread[:, lanes]).astype(bf16)
        at += here.shape[1]


def to_planes(src, dst, height):
    for s in range(tiles - 1):
        dst[pl.ds(s * height, height), :] = src[:, s * 128 : (s + 1) * 128].astype(f32)
    last = src[:, (tiles - 1) * 128 :].astype(f32)
    if last.shape[1] < 128:
        last = jnp.concatenate([last, jnp.zeros((height, 128 - last.shape[1]), f32)], 1)
    dst[pl.ds((tiles - 1) * height, height), :] = last


def every_eighth(planes, height, child, count):
    parts = [planes[pl.ds(s * height + child, count, stride=8), :] for s in range(tiles)]
    return jnp.concatenate(parts, 1).astype(bf16)


def up_kernel(sc, ops, other, *refs):
    mine, o_ref, op_planes, box_planes = refs[:-3], refs[-3], refs[-2], refs[-1]
    to_planes(ops, op_planes, 8 * share)
    for s in range(tiles):
        lanes = slice(s * 128, (s + 1) * 128)
        for i, part in enumerate(mine):
            at = pl.multiple_of(s * boxes + sc[0] * half + i * chunk, chunk)
            box_planes[pl.ds(at, chunk), :] = part[:, lanes].astype(f32)
        at = pl.multiple_of(s * boxes + (1 - sc[0]) * half, half)
        box_planes[pl.ds(at, half), :] = other[:, lanes].astype(f32)
    total = None
    for child in range(8):
        left = every_eighth(op_planes, 8 * share, child, share)
        right = every_eighth(box_planes, boxes, child, parents)
        term = lax.dot_general(left, right, (((1,), (1,)), ((), ())), preferred_element_type=f32)
        total = term if total is None else total + term
    o_ref[...] = total.astype(bf16)


def parent_rows(sc, ops, mine, other):
    args = (ops, other, *mine)
    return call(
        up_kernel,
        sc,
        args,
        [whole(a) for a in args],
        whole(),
        jax.ShapeDtypeStruct((share, parents), bf16),
        14,
        scratch=[
            pltpu.VMEM((tiles * 8 * share, 128), f32),
            pltpu.VMEM((tiles * boxes, 128), f32),
        ],
    )


def coarse_kernel(sc, lists, far, own, a, b, own_o, ab_o, send, keep, picked, result):
    c, l = sc[0], sc[1]
    wanted = jnp.concatenate([lists[k : k + 1, :] for k in range(3)], 1)
    count = wanted.shape[1]
    spot = lax.broadcasted_iota(jnp.int32, (parents, count), 0)
    hot = jnp.concatenate(
        [
            (spot == wanted - base).astype(f32).astype(bf16)
            for base in (parents, sc[2], sc[3])
        ],
        0,
    )

    def pick(*parts):
        return jnp.dot(jnp.concatenate(parts, 1), hot, preferred_element_type=f32)

    lo, hi = slice(0, parents), slice(parents, 2 * parents)
    a_o, b_o = ab_o[:, : 2 * parents], ab_o[:, 2 * parents :]
    found = (
        (pick(own[:, lo], a[:, hi], b[:, lo]), pick(own[:, hi], a[:, lo], b[:, hi])),
        (pick(own_o[:, lo], a_o[:, hi], b_o[:, lo]), pick(own_o[:, hi], a_o[:, lo], b_o[:, hi])),
    )
    for j in range(4):
        x, y = j // 2, j % 2
        mine = jnp.where(l == x, found[0][0], found[0][1])
        theirs = jnp.where(l == x, found[1][0], found[1][1])
        picked[pl.ds(share * j, share), :] = jnp.where(c == y, mine, theirs)
    sources = picked[...].astype(bf16)
    total = None
    for k in range(3):
        term = jnp.dot(
            far[k], sources[:, k * parents : (k + 1) * parents], preferred_element_type=f32
        )
        total = term if total is None else total + term
    result[pl.ds(0, rows), :] = total * coarse_scale
    result[pl.ds(rows, wide - rows), :] = jnp.zeros((wide - rows, parents), f32)
    part = wide // 2
    keep[...] = result[pl.ds(pl.multiple_of(c * part, part), part), :]
    send[...] = result[pl.ds(pl.multiple_of((1 - c) * part, part), part), :].astype(bf16)


def coarse_partial(sc, lists, far, own, a, b, own_o, ab_o):
    args = (lists, far, own, a, b, own_o, ab_o)
    shape = (wide // 2, parents)
    return call(
        coarse_kernel,
        sc,
        args,
        [whole(x) for x in args],
        [whole(), whole()],
        [jax.ShapeDtypeStruct(shape, bf16), jax.ShapeDtypeStruct(shape, f32)],
        8,
        scratch=[pltpu.VMEM((rows, 3 * parents), f32), pltpu.VMEM((wide, parents), f32)],
    )


def down_kernel(sc, ops, mine, other, o_ref, op_planes, check, turned_rows):
    c, part = sc[0], wide // 2
    to_planes(ops, op_planes, 8 * share)
    check[pl.ds(pl.multiple_of(c * part, part), part), :] = mine[...]
    check[pl.ds(pl.multiple_of((1 - c) * part, part), part), :] = other[...]
    whole_check = check[...]
    for child in range(8):
        left = every_eighth(op_planes, 8 * share, child, share)
        z = jnp.dot(left, whole_check, preferred_element_type=f32)
        z = jnp.concatenate([z, jnp.zeros((256 - share, parents), f32)], 0).T
        for t in (0, 1):
            turned_rows[pl.ds(t * boxes + child, parents, stride=8), :] = z[
                :, t * 128 : (t + 1) * 128
            ]
    o_ref[pl.ds(0, 128), :] = turned_rows[pl.ds(0, boxes), :].T
    o_ref[pl.ds(128, share - 128), :] = turned_rows[pl.ds(boxes, boxes), :].T[: share - 128]


def downward(sc, ops, mine, other):
    args = (ops, mine, other)
    return call(
        down_kernel,
        sc,
        args,
        [whole(x) for x in args],
        whole(),
        jax.ShapeDtypeStruct((share, boxes), f32),
        12,
        scratch=[
            pltpu.VMEM((tiles * 8 * share, 128), f32),
            pltpu.VMEM((wide, parents), bf16),
            pltpu.VMEM((2 * boxes, 128), f32),
        ],
    )


pitch, step_boxes, unroll = early + 8, 512, 32


def gather_kernel(spots, *refs):
    pieces, o_ref, planes, got = refs[:-3], refs[-3], refs[-2], refs[-1]
    step = pl.program_id(0)
    depth = step_boxes + 8
    entry = step // (boxes // step_boxes)
    first = (step % (boxes // step_boxes)) * step_boxes

    @pl.when(step == 0)
    def _():
        at = 0
        for piece in pieces:
            count = piece.shape[0]
            for s in range(tiles):
                planes[pl.ds(s * pitch + at, count), :] = piece[
                    :, s * 128 : (s + 1) * 128
                ].astype(f32)
            at += count
        for s in range(tiles):
            planes[pl.ds(s * pitch + early, 8), :] = jnp.zeros((8, 128), f32)

    def body(i, carry):
        found = [
            planes[pl.ds(spots[entry, first + i * unroll + u], 8, stride=pitch), :]
            for u in range(unroll)
        ]
        for u in range(unroll):
            got[pl.ds(i * unroll + u, 8, stride=depth), :] = found[u]
        return carry

    lax.fori_loop(0, step_boxes // unroll, body, 0)
    for s in range(tiles):
        spot = pl.ds(pl.multiple_of(step * step_boxes, step_boxes), step_boxes)
        o_ref[spot, s * 128 : (s + 1) * 128] = got[pl.ds(s * depth, step_boxes), :].astype(bf16)


def gathered(spots, pieces):
    return call(
        gather_kernel,
        spots,
        tuple(pieces),
        [whole(p) for p in pieces],
        whole(),
        jax.ShapeDtypeStruct((3 * boxes, wide), bf16),
        16,
        grid=(3 * boxes // step_boxes,),
        scratch=[
            pltpu.VMEM((8 * pitch, 128), f32),
            pltpu.VMEM((8 * (step_boxes + 8), 128), f32),
        ],
    )


def far_kernel(start, width, sc, far, sources, lists, late, late_o, send, keep, result):
    c = sc[0]
    spot = lax.broadcasted_iota(jnp.int32, (width, 128), 1).astype(f32)
    late_boxes = jnp.concatenate([late[...], late_o[...]], 0)

    def tile(i):
        total = None
        for k in range(3):
            at = k * boxes + start + i * width
            wanted = jnp.broadcast_to(lists[k : k + 1, pl.ds(start + i * width, width)].astype(f32), (128, width)).T
            hot = jnp.concatenate(
                [
                    (wanted == spot + float(base)).astype(f32).astype(bf16)
                    for base in range(0, 2 * chunk, 128)
                ],
                1,
            )
            found = jnp.dot(hot, late_boxes, preferred_element_type=f32)
            found = found + sources[pl.ds(at, width), :].astype(f32)
            term = lax.dot_general(
                far[k],
                found.astype(bf16)[:, :rows],
                (((1,), (1,)), ((), ())),
                preferred_element_type=f32,
            )
            total = term if total is None else total + term
        result[...] = total
        lanes = pl.ds(i * width, width)
        for x in (0, 1):
            first = result[pl.ds(share * 2 * x, share), :]
            second = result[pl.ds(share * (2 * x + 1), share), :]
            keep[x, :, lanes] = jnp.where(c == 0, first, second)
            send[x, :, lanes] = jnp.where(c == 0, second, first).astype(bf16)

    for i in range(send.shape[2] // width):
        tile(i)


def far_partial(sc, far, sources, lists, late, late_o, start, count, width=256):
    shape = (2, share, count)
    args = (far, sources, lists, late, late_o)
    return call(
        functools.partial(far_kernel, start, width),
        sc,
        args,
        [whole(x) for x in args],
        [whole(), whole()],
        [jax.ShapeDtypeStruct(shape, bf16), jax.ShapeDtypeStruct(shape, f32)],
        12,
        scratch=[pltpu.VMEM((rows, width), f32)],
    )


def after(x, *others):
    return lax.optimization_barrier((x, *others))[0]


def local(leaf_density, upward_ops, far_ops, downward_ops, fine_lists, coarse_lists):
    groups = lax.axis_size("space")
    group, rep = lax.axis_index("space"), lax.axis_index("rep")
    l, c = rep >> 1, rep & 1
    no_previous, no_next = group == 0, group == groups - 1
    nowhere = -16384
    base_previous = jnp.where(no_previous, nowhere, 0)
    base_next = jnp.where(no_next, nowhere, 2 * parents)
    sc = jnp.stack(
        [
            c,
            l,
            jnp.where(l == 0, base_previous, base_next),
            jnp.where(l == 0, base_next, base_previous),
        ]
    ).astype(jnp.int32)
    hop = functools.partial(lax.ppermute, axis_name=both, perm=one_hop(groups))
    zswap = functools.partial(lax.ppermute, axis_name=both, perm=across(groups, 2))
    cswap = functools.partial(lax.ppermute, axis_name=both, perm=across(groups, 1))

    def at(i):
        return jnp.reshape(i, (1,)).astype(jnp.int32)

    up_ops = jnp.transpose(upward_ops, (1, 0, 2)).reshape(8 * share, rows)
    down_ops = jnp.transpose(downward_ops, (1, 0, 2)).reshape(8 * share, rows)

    which, side, offset = fine_lists >> 10, (fine_lists >> 9) & 1, fine_lists & (half - 1)
    outside = ((which == 0) & no_previous) | ((which == 2) & no_next)
    direct = (which == 0) == (l == 0)
    theirs = (side != c).astype(jnp.int32)
    is_late = (which != 1) & ~direct & (offset >= half - chunk)
    spots = jnp.where(
        which == 1,
        theirs * half + offset,
        jnp.where(
            direct,
            2 * half + theirs * half + offset,
            4 * half + theirs * (half - chunk) + offset,
        ),
    )
    spots = jnp.where(outside | is_late, early, spots)
    late_lists = jnp.where(is_late & ~outside, theirs * chunk + offset - (half - chunk), -1)

    head = turned(leaf_density, at(c * half), [chunk])[0]
    rest = jnp.stack([c * half + chunk, (1 - c) * half]).astype(jnp.int32)
    tail, other = turned(leaf_density, after(rest, head), [half - chunk, half])
    up = parent_rows(after(sc, spots, late_lists), up_ops, [head, tail], other)
    mine = [head, after(tail, up)]
    a = [hop(m) for m in mine]
    own = joined(sc, up, zswap(up))
    early_a = after(a[0], up)
    b = [zswap(early_a)]
    a_o = [cswap(early_a)]
    ca = hop(own)
    own_o = cswap(own)
    second = after(a[1], early_a, ca, own_o)
    b.append(zswap(second))
    a_o.append(cswap(second))
    cb = zswap(ca)
    b_o = [cswap(b[0])]
    picked = gathered(spots, [*mine, other, *a, *a_o, b[0], b_o[0]])
    b_o.append(cswap(after(b[1], picked)))
    cab_o = cswap(joined(sc, ca, cb))

    def summed(send, keep):
        shape = (share, send.shape[2])
        here, away = small(split_kernel, sc, (keep, cswap(send)), [(shape, f32), (shape, bf16)])
        return here, zswap(away), away

    late = (b[1], b_o[1])
    send, keep = far_partial(sc, far_ops, picked, late_lists, *late, 0, half)
    left = summed(after(send, cb), keep)
    send, keep = coarse_partial(after(sc, send), coarse_lists, far_ops, own, ca, cb, own_o, cab_o)
    shape = (wide // 2, parents)
    part, part_sent = small(add_kernel, sc, (keep, cswap(send)), [(shape, f32), (shape, bf16)])
    send, keep = far_partial(
        after(sc, part, left[2]), far_ops, picked, late_lists, *late, half, half
    )
    part_got = zswap(part_sent)
    right = summed(after(send, left[1], part_got), keep)
    check = small(add_kernel, sc, (part, part_got), [(shape, bf16)])[0]
    spread = downward(after(sc, right[2]), down_ops, check, cswap(check))
    return small(last_kernel, sc, (spread, *left[:2], *right[:2]), [((share, boxes), bf16)])[0]


def solution(mesh):
    return jax.shard_map(
        local,
        mesh=mesh,
        in_specs=(
            P(None, "space"),
            P(None, "rep", None),
            P("rep", None, None),
            P(None, "rep", None),
            P("rep", "space"),
            P("rep", "space"),
        ),
        out_specs=P("rep", "space"),
        check_vma=False,
    )
```

```python
import functools

import jax
import jax.numpy as jnp
from jax import lax
from jax.experimental import pallas as pl
from jax.experimental.pallas import tpu as pltpu
from jax.sharding import PartitionSpec as P

bf16, f32 = jnp.bfloat16, jnp.float32
both = ("space", "rep")
coarse_scale = 0.5
rows, wide, tiles = 888, 896, 7
boxes, half = 1024, 512
parents = 128
share = 222
chunks = 2
chunk = half // chunks
early = 6 * half - 2 * chunk


def one_hop(groups):
    up = [(4 * s + 2 + c, 4 * (s + 1) + c) for s in range(groups - 1) for c in (0, 1)]
    ends = [(i, i) for i in (0, 1, 4 * groups - 2, 4 * groups - 1)]
    return up + [(j, i) for i, j in up] + ends


def across(groups, flip):
    return [(4 * s + r, 4 * s + (r ^ flip)) for s in range(groups) for r in range(4)]


def call(kernel, scalars, args, in_specs, out_specs, out_shape, limit, grid=(1,), scratch=()):
    return pl.pallas_call(
        kernel,
        grid_spec=pltpu.PrefetchScalarGridSpec(
            num_scalar_prefetch=1,
            grid=grid,
            in_specs=in_specs,
            out_specs=out_specs,
            scratch_shapes=scratch,
        ),
        out_shape=out_shape,
        compiler_params=pltpu.CompilerParams(vmem_limit_bytes=limit << 20),
        cost_estimate=pl.CostEstimate(flops=0, bytes_accessed=0, transcendentals=0),
    )(scalars, *args)


def whole(a=None):
    return pl.BlockSpec(memory_space=pltpu.VMEM)


def turn_kernel(firsts, x_ref, *outs):
    for n, o_ref in enumerate(outs):
        for i in range(o_ref.shape[0] // 128):
            part = x_ref[:, pl.ds(pl.multiple_of(firsts[n] + i * 128, 128), 128)].astype(f32)
            tall = jnp.concatenate([part, jnp.zeros((wide - rows, 128), f32)], 0)
            o_ref[pl.ds(i * 128, 128), :] = tall.T.astype(bf16)


def turned(x, firsts, counts):
    shapes = [jax.ShapeDtypeStruct((n, wide), bf16) for n in counts]
    return call(turn_kernel, firsts, (x,), [whole()], [whole() for _ in counts], shapes, 8)


def small(kernel, sc, args, shapes, limit=6):
    shapes = [jax.ShapeDtypeStruct(*s) for s in shapes]
    return call(kernel, sc, args, [whole() for _ in args], [whole() for _ in shapes], shapes, limit)


def join_kernel(sc, *refs):
    at = 0
    for part in refs[:-1]:
        refs[-1][:, at : at + part.shape[1]] = part[...]
        at += part.shape[1]


def joined(sc, *parts):
    width = sum(p.shape[1] for p in parts)
    return small(join_kernel, sc, parts, [((parts[0].shape[0], width), bf16)])[0]


def split_kernel(sc, keep, got, here, away):
    l = sc[1]
    here[...] = keep[l] + got[l].astype(f32)
    away[...] = (keep[1 - l] + got[1 - l].astype(f32)).astype(bf16)


def add_kernel(sc, one, two, *outs):
    total = one[...] + two[...].astype(f32)
    for o_ref in outs:
        o_ref[...] = total.astype(o_ref.dtype)


def last_kernel(sc, spread, *refs):
    o_ref, at = refs[-1], 0
    for here, there in zip(refs[:-1:2], refs[1:-1:2]):
        lanes = slice(at, at + here.shape[1])
        o_ref[:, lanes] = (here[...] + there[...].astype(f32) + spread[:, lanes]).astype(bf16)
        at += here.shape[1]


def to_planes(src, dst, height):
    for s in range(tiles - 1):
        dst[pl.ds(s * height, height), :] = src[:, s * 128 : (s + 1) * 128].astype(f32)
    last = src[:, (tiles - 1) * 128 :].astype(f32)
    if last.shape[1] < 128:
        last = jnp.concatenate([last, jnp.zeros((height, 128 - last.shape[1]), f32)], 1)
    dst[pl.ds((tiles - 1) * height, height), :] = last


def every_eighth(planes, height, child, count):
    parts = [planes[pl.ds(s * height + child, count, stride=8), :] for s in range(tiles)]
    return jnp.concatenate(parts, 1).astype(bf16)


def up_kernel(sc, ops, other, *refs):
    mine, o_ref, op_planes, box_planes = refs[:-3], refs[-3], refs[-2], refs[-1]
    to_planes(ops, op_planes, 8 * share)
    for s in range(tiles):
        lanes = slice(s * 128, (s + 1) * 128)
        for i, part in enumerate(mine):
            at = pl.multiple_of(s * boxes + sc[0] * half + i * chunk, chunk)
            box_planes[pl.ds(at, chunk), :] = part[:, lanes].astype(f32)
        at = pl.multiple_of(s * boxes + (1 - sc[0]) * half, half)
        box_planes[pl.ds(at, half), :] = other[:, lanes].astype(f32)
    total = None
    for child in range(8):
        left = every_eighth(op_planes, 8 * share, child, share)
        right = every_eighth(box_planes, boxes, child, parents)
        term = lax.dot_general(left, right, (((1,), (1,)), ((), ())), preferred_element_type=f32)
        total = term if total is None else total + term
    o_ref[...] = total.astype(bf16)


def parent_rows(sc, ops, mine, other):
    args = (ops, other, *mine)
    return call(
        up_kernel,
        sc,
        args,
        [whole(a) for a in args],
        whole(),
        jax.ShapeDtypeStruct((share, parents), bf16),
        14,
        scratch=[
            pltpu.VMEM((tiles * 8 * share, 128), f32),
            pltpu.VMEM((tiles * boxes, 128), f32),
        ],
    )


def coarse_kernel(sc, lists, far, own, a, b, own_o, ab_o, send, keep, picked, result):
    c, l = sc[0], sc[1]
    wanted = jnp.concatenate([lists[k : k + 1, :] for k in range(3)], 1)
    count = wanted.shape[1]
    spot = lax.broadcasted_iota(jnp.int32, (parents, count), 0)
    hot = jnp.concatenate(
        [
            (spot == wanted - base).astype(f32).astype(bf16)
            for base in (parents, sc[2], sc[3])
        ],
        0,
    )

    def pick(*parts):
        return jnp.dot(jnp.concatenate(parts, 1), hot, preferred_element_type=f32)

    lo, hi = slice(0, parents), slice(parents, 2 * parents)
    a_o, b_o = ab_o[:, : 2 * parents], ab_o[:, 2 * parents :]
    found = (
        (pick(own[:, lo], a[:, hi], b[:, lo]), pick(own[:, hi], a[:, lo], b[:, hi])),
        (pick(own_o[:, lo], a_o[:, hi], b_o[:, lo]), pick(own_o[:, hi], a_o[:, lo], b_o[:, hi])),
    )
    for j in range(4):
        x, y = j // 2, j % 2
        mine = jnp.where(l == x, found[0][0], found[0][1])
        theirs = jnp.where(l == x, found[1][0], found[1][1])
        picked[pl.ds(share * j, share), :] = jnp.where(c == y, mine, theirs)
    sources = picked[...].astype(bf16)
    total = None
    for k in range(3):
        term = jnp.dot(
            far[k], sources[:, k * parents : (k + 1) * parents], preferred_element_type=f32
        )
        total = term if total is None else total + term
    result[pl.ds(0, rows), :] = total * coarse_scale
    result[pl.ds(rows, wide - rows), :] = jnp.zeros((wide - rows, parents), f32)
    part = wide // 2
    keep[...] = result[pl.ds(pl.multiple_of(c * part, part), part), :]
    send[...] = result[pl.ds(pl.multiple_of((1 - c) * part, part), part), :].astype(bf16)


def coarse_partial(sc, lists, far, own, a, b, own_o, ab_o):
    args = (lists, far, own, a, b, own_o, ab_o)
    shape = (wide // 2, parents)
    return call(
        coarse_kernel,
        sc,
        args,
        [whole(x) for x in args],
        [whole(), whole()],
        [jax.ShapeDtypeStruct(shape, bf16), jax.ShapeDtypeStruct(shape, f32)],
        8,
        scratch=[pltpu.VMEM((rows, 3 * parents), f32), pltpu.VMEM((wide, parents), f32)],
    )


def down_kernel(sc, ops, mine, other, o_ref, op_planes, check, turned_rows):
    c, part = sc[0], wide // 2
    to_planes(ops, op_planes, 8 * share)
    check[pl.ds(pl.multiple_of(c * part, part), part), :] = mine[...]
    check[pl.ds(pl.multiple_of((1 - c) * part, part), part), :] = other[...]
    whole_check = check[...]
    for child in range(8):
        left = every_eighth(op_planes, 8 * share, child, share)
        z = jnp.dot(left, whole_check, preferred_element_type=f32)
        z = jnp.concatenate([z, jnp.zeros((256 - share, parents), f32)], 0).T
        for t in (0, 1):
            turned_rows[pl.ds(t * boxes + child, parents, stride=8), :] = z[
                :, t * 128 : (t + 1) * 128
            ]
    o_ref[pl.ds(0, 128), :] = turned_rows[pl.ds(0, boxes), :].T
    o_ref[pl.ds(128, share - 128), :] = turned_rows[pl.ds(boxes, boxes), :].T[: share - 128]


def downward(sc, ops, mine, other):
    args = (ops, mine, other)
    return call(
        down_kernel,
        sc,
        args,
        [whole(x) for x in args],
        whole(),
        jax.ShapeDtypeStruct((share, boxes), f32),
        12,
        scratch=[
            pltpu.VMEM((tiles * 8 * share, 128), f32),
            pltpu.VMEM((wide, parents), bf16),
            pltpu.VMEM((2 * boxes, 128), f32),
        ],
    )


pitch, step_boxes, unroll = early + 8, 512, 32


def gather_kernel(spots, *refs):
    pieces, o_ref, planes, got = refs[:-3], refs[-3], refs[-2], refs[-1]
    step = pl.program_id(0)
    depth = step_boxes + 8

    @pl.when(step == 0)
    def _():
        at = 0
        for piece in pieces:
            count = piece.shape[0]
            for s in range(tiles):
                planes[pl.ds(s * pitch + at, count), :] = piece[
                    :, s * 128 : (s + 1) * 128
                ].astype(f32)
            at += count
        for s in range(tiles):
            planes[pl.ds(s * pitch + early, 8), :] = jnp.zeros((8, 128), f32)

    def body(i, carry):
        found = [
            planes[pl.ds(spots[step * step_boxes + i * unroll + u], 8, stride=pitch), :]
            for u in range(unroll)
        ]
        for u in range(unroll):
            got[pl.ds(i * unroll + u, 8, stride=depth), :] = found[u]
        return carry

    lax.fori_loop(0, step_boxes // unroll, body, 0)
    for s in range(tiles):
        spot = pl.ds(pl.multiple_of(step * step_boxes, step_boxes), step_boxes)
        o_ref[spot, s * 128 : (s + 1) * 128] = got[pl.ds(s * depth, step_boxes), :].astype(bf16)


def gathered(spots, pieces):
    return call(
        gather_kernel,
        spots,
        tuple(pieces),
        [whole(p) for p in pieces],
        whole(),
        jax.ShapeDtypeStruct((3 * boxes, wide), bf16),
        16,
        grid=(3 * boxes // step_boxes,),
        scratch=[
            pltpu.VMEM((8 * pitch, 128), f32),
            pltpu.VMEM((8 * (step_boxes + 8), 128), f32),
        ],
    )


def far_kernel(start, width, sc, far, sources, lists, late, late_o, send, keep, result):
    c = sc[0]
    spot = lax.broadcasted_iota(jnp.int32, (width, 128), 1).astype(f32)
    late_boxes = jnp.concatenate([late[...], late_o[...]], 0)

    def tile(i):
        total = None
        for k in range(3):
            at = k * boxes + start + i * width
            wanted = jnp.broadcast_to(lists[k : k + 1, pl.ds(start + i * width, width)].astype(f32), (128, width)).T
            hot = jnp.concatenate(
                [
                    (wanted == spot + float(base)).astype(f32).astype(bf16)
                    for base in range(0, 2 * chunk, 128)
                ],
                1,
            )
            found = jnp.dot(hot, late_boxes, preferred_element_type=f32)
            found = found + sources[pl.ds(at, width), :].astype(f32)
            term = lax.dot_general(
                far[k],
                found.astype(bf16)[:, :rows],
                (((1,), (1,)), ((), ())),
                preferred_element_type=f32,
            )
            total = term if total is None else total + term
        result[...] = total
        lanes = pl.ds(i * width, width)
        for x in (0, 1):
            first = result[pl.ds(share * 2 * x, share), :]
            second = result[pl.ds(share * (2 * x + 1), share), :]
            keep[x, :, lanes] = jnp.where(c == 0, first, second)
            send[x, :, lanes] = jnp.where(c == 0, second, first).astype(bf16)

    for i in range(send.shape[2] // width):
        tile(i)


def far_partial(sc, far, sources, lists, late, late_o, start, count, width=256):
    shape = (2, share, count)
    args = (far, sources, lists, late, late_o)
    return call(
        functools.partial(far_kernel, start, width),
        sc,
        args,
        [whole(x) for x in args],
        [whole(), whole()],
        [jax.ShapeDtypeStruct(shape, bf16), jax.ShapeDtypeStruct(shape, f32)],
        12,
        scratch=[pltpu.VMEM((rows, width), f32)],
    )


def after(x, *others):
    return lax.optimization_barrier((x, *others))[0]


def local(leaf_density, upward_ops, far_ops, downward_ops, fine_lists, coarse_lists):
    groups = lax.axis_size("space")
    group, rep = lax.axis_index("space"), lax.axis_index("rep")
    l, c = rep >> 1, rep & 1
    no_previous, no_next = group == 0, group == groups - 1
    nowhere = -16384
    base_previous = jnp.where(no_previous, nowhere, 0)
    base_next = jnp.where(no_next, nowhere, 2 * parents)
    sc = jnp.stack(
        [
            c,
            l,
            jnp.where(l == 0, base_previous, base_next),
            jnp.where(l == 0, base_next, base_previous),
        ]
    ).astype(jnp.int32)
    hop = functools.partial(lax.ppermute, axis_name=both, perm=one_hop(groups))
    zswap = functools.partial(lax.ppermute, axis_name=both, perm=across(groups, 2))
    cswap = functools.partial(lax.ppermute, axis_name=both, perm=across(groups, 1))

    def at(i):
        return jnp.reshape(i, (1,)).astype(jnp.int32)

    up_ops = jnp.transpose(upward_ops, (1, 0, 2)).reshape(8 * share, rows)
    down_ops = jnp.transpose(downward_ops, (1, 0, 2)).reshape(8 * share, rows)

    which, side, offset = fine_lists >> 10, (fine_lists >> 9) & 1, fine_lists & (half - 1)
    outside = ((which == 0) & no_previous) | ((which == 2) & no_next)
    direct = (which == 0) == (l == 0)
    theirs = (side != c).astype(jnp.int32)
    is_late = (which != 1) & ~direct & (offset >= half - chunk)
    spots = jnp.where(
        which == 1,
        theirs * half + offset,
        jnp.where(
            direct,
            2 * half + theirs * half + offset,
            4 * half + theirs * (half - chunk) + offset,
        ),
    )
    spots = jnp.where(outside | is_late, early, spots).reshape(-1)
    late_lists = jnp.where(is_late & ~outside, theirs * chunk + offset - (half - chunk), -1)

    head = turned(leaf_density, at(c * half), [chunk])[0]
    rest = jnp.stack([c * half + chunk, (1 - c) * half]).astype(jnp.int32)
    tail, other = turned(leaf_density, after(rest, head), [half - chunk, half])
    up = parent_rows(after(sc, spots, late_lists), up_ops, [head, tail], other)
    mine = [head, after(tail, up)]
    a = [hop(m) for m in mine]
    own = joined(sc, up, zswap(up))
    early_a = after(a[0], own)
    b = [zswap(early_a)]
    a_o = [cswap(early_a)]
    ca = hop(own)
    own_o = cswap(own)
    second = after(a[1], early_a, ca, own_o)
    b.append(zswap(second))
    a_o.append(cswap(second))
    cb = zswap(ca)
    b_o = [cswap(b[0])]
    picked = gathered(spots, [*mine, other, *a, *a_o, b[0], b_o[0]])
    b_o.append(cswap(after(b[1], picked)))
    cab_o = cswap(joined(sc, ca, cb))

    def summed(send, keep):
        shape = (share, send.shape[2])
        here, away = small(split_kernel, sc, (keep, cswap(send)), [(shape, f32), (shape, bf16)])
        return here, zswap(away), away

    late = (b[1], b_o[1])
    send, keep = far_partial(sc, far_ops, picked, late_lists, *late, 0, half)
    left = summed(after(send, cb), keep)
    send, keep = coarse_partial(after(sc, send), coarse_lists, far_ops, own, ca, cb, own_o, cab_o)
    shape = (wide // 2, parents)
    part, part_sent = small(add_kernel, sc, (keep, cswap(send)), [(shape, f32), (shape, bf16)])
    send, keep = far_partial(
        after(sc, part, left[2]), far_ops, picked, late_lists, *late, half, half
    )
    part_got = zswap(part_sent)
    right = summed(after(send, left[1], part_got), keep)
    check = small(add_kernel, sc, (part, part_got), [(shape, bf16)])[0]
    spread = downward(after(sc, right[2]), down_ops, check, cswap(check))
    return small(last_kernel, sc, (spread, *left[:2], *right[:2]), [((share, boxes), bf16)])[0]


def solution(mesh):
    return jax.shard_map(
        local,
        mesh=mesh,
        in_specs=(
            P(None, "space"),
            P(None, "rep", None),
            P("rep", None, None),
            P(None, "rep", None),
            P("rep", "space"),
            P("rep", "space"),
        ),
        out_specs=P("rep", "space"),
        check_vma=False,
    )
```

```python
import functools

import jax
import jax.numpy as jnp
from jax import lax
from jax.experimental import pallas as pl
from jax.experimental.pallas import tpu as pltpu
from jax.sharding import PartitionSpec as P

bf16, f32 = jnp.bfloat16, jnp.float32
both = ("space", "rep")
coarse_scale = 0.5
rows, wide, tiles = 888, 896, 7
boxes, half = 1024, 512
parents = 128
share = 222
chunks = 2
chunk = half // chunks
early = 6 * half - 2 * chunk
ahead = 640


def one_hop(groups):
    up = [(4 * s + 2 + c, 4 * (s + 1) + c) for s in range(groups - 1) for c in (0, 1)]
    up += [(0, 1), (4 * groups - 2, 4 * groups - 1)]
    return up + [(j, i) for i, j in up]


def across(groups, flip):
    return [(4 * s + r, 4 * s + (r ^ flip)) for s in range(groups) for r in range(4)]


def call(kernel, scalars, args, in_specs, out_specs, out_shape, limit, grid=(1,), scratch=()):
    return pl.pallas_call(
        kernel,
        grid_spec=pltpu.PrefetchScalarGridSpec(
            num_scalar_prefetch=1,
            grid=grid,
            in_specs=in_specs,
            out_specs=out_specs,
            scratch_shapes=scratch,
        ),
        out_shape=out_shape,
        compiler_params=pltpu.CompilerParams(vmem_limit_bytes=limit << 20),
        cost_estimate=pl.CostEstimate(flops=0, bytes_accessed=0, transcendentals=0),
    )(scalars, *args)


def whole(a=None):
    return pl.BlockSpec(memory_space=pltpu.VMEM)


def turn_kernel(firsts, x_ref, *outs):
    for n, o_ref in enumerate(outs):
        for i in range(o_ref.shape[0] // 128):
            part = x_ref[:, pl.ds(pl.multiple_of(firsts[n] + i * 128, 128), 128)].astype(f32)
            tall = jnp.concatenate([part, jnp.zeros((wide - rows, 128), f32)], 0)
            o_ref[pl.ds(i * 128, 128), :] = tall.T.astype(bf16)


def turned(x, firsts, counts):
    shapes = [jax.ShapeDtypeStruct((n, wide), bf16) for n in counts]
    return call(turn_kernel, firsts, (x,), [whole()], [whole() for _ in counts], shapes, 8)


def small(kernel, sc, args, shapes, limit=6):
    shapes = [jax.ShapeDtypeStruct(*s) for s in shapes]
    return call(kernel, sc, args, [whole() for _ in args], [whole() for _ in shapes], shapes, limit)


def join_kernel(sc, *refs):
    at = 0
    for part in refs[:-1]:
        refs[-1][:, at : at + part.shape[1]] = part[...]
        at += part.shape[1]


def joined(sc, *parts):
    width = sum(p.shape[1] for p in parts)
    return small(join_kernel, sc, parts, [((parts[0].shape[0], width), bf16)])[0]


def split_kernel(sc, keep, got, here, away):
    l = sc[1]
    here[...] = keep[l] + got[l].astype(f32)
    away[...] = (keep[1 - l] + got[1 - l].astype(f32)).astype(bf16)


def add_kernel(sc, one, two, *outs):
    total = one[...] + two[...].astype(f32)
    for o_ref in outs:
        o_ref[...] = total.astype(o_ref.dtype)


def last_kernel(sc, spread, *refs):
    o_ref, at = refs[-1], 0
    for here, there in zip(refs[:-1:2], refs[1:-1:2]):
        lanes = slice(at, at + here.shape[1])
        o_ref[:, lanes] = (here[...] + there[...].astype(f32) + spread[:, lanes]).astype(bf16)
        at += here.shape[1]


def to_planes(src, dst, height):
    for s in range(tiles - 1):
        dst[pl.ds(s * height, height), :] = src[:, s * 128 : (s + 1) * 128].astype(f32)
    last = src[:, (tiles - 1) * 128 :].astype(f32)
    if last.shape[1] < 128:
        last = jnp.concatenate([last, jnp.zeros((height, 128 - last.shape[1]), f32)], 1)
    dst[pl.ds((tiles - 1) * height, height), :] = last


def every_eighth(planes, height, child, count):
    parts = [planes[pl.ds(s * height + child, count, stride=8), :] for s in range(tiles)]
    return jnp.concatenate(parts, 1).astype(bf16)


def up_kernel(sc, ops, other, *refs):
    mine, o_ref, op_planes, box_planes = refs[:-3], refs[-3], refs[-2], refs[-1]
    to_planes(ops, op_planes, 8 * share)
    for s in range(tiles):
        lanes = slice(s * 128, (s + 1) * 128)
        for i, part in enumerate(mine):
            at = pl.multiple_of(s * boxes + sc[0] * half + i * chunk, chunk)
            box_planes[pl.ds(at, chunk), :] = part[:, lanes].astype(f32)
        at = pl.multiple_of(s * boxes + (1 - sc[0]) * half, half)
        box_planes[pl.ds(at, half), :] = other[:, lanes].astype(f32)
    total = None
    for child in range(8):
        left = every_eighth(op_planes, 8 * share, child, share)
        right = every_eighth(box_planes, boxes, child, parents)
        term = lax.dot_general(left, right, (((1,), (1,)), ((), ())), preferred_element_type=f32)
        total = term if total is None else total + term
    o_ref[...] = total.astype(bf16)


def parent_rows(sc, ops, mine, other):
    args = (ops, other, *mine)
    return call(
        up_kernel,
        sc,
        args,
        [whole(a) for a in args],
        whole(),
        jax.ShapeDtypeStruct((share, parents), bf16),
        14,
        scratch=[
            pltpu.VMEM((tiles * 8 * share, 128), f32),
            pltpu.VMEM((tiles * boxes, 128), f32),
        ],
    )


def coarse_kernel(sc, lists, far, own, a, b, own_o, ab_o, send, keep, picked, result):
    c, l = sc[0], sc[1]
    wanted = jnp.concatenate([lists[k : k + 1, :] for k in range(3)], 1)
    count = wanted.shape[1]
    spot = lax.broadcasted_iota(jnp.int32, (parents, count), 0)
    hot = jnp.concatenate(
        [
            (spot == wanted - base).astype(f32).astype(bf16)
            for base in (parents, sc[2], sc[3])
        ],
        0,
    )

    def pick(*parts):
        return jnp.dot(jnp.concatenate(parts, 1), hot, preferred_element_type=f32)

    lo, hi = slice(0, parents), slice(parents, 2 * parents)
    a_o, b_o = ab_o[:, : 2 * parents], ab_o[:, 2 * parents :]
    found = (
        (pick(own[:, lo], a[:, hi], b[:, lo]), pick(own[:, hi], a[:, lo], b[:, hi])),
        (pick(own_o[:, lo], a_o[:, hi], b_o[:, lo]), pick(own_o[:, hi], a_o[:, lo], b_o[:, hi])),
    )
    for j in range(4):
        x, y = j // 2, j % 2
        mine = jnp.where(l == x, found[0][0], found[0][1])
        theirs = jnp.where(l == x, found[1][0], found[1][1])
        picked[pl.ds(share * j, share), :] = jnp.where(c == y, mine, theirs)
    sources = picked[...].astype(bf16)
    total = None
    for k in range(3):
        term = jnp.dot(
            far[k], sources[:, k * parents : (k + 1) * parents], preferred_element_type=f32
        )
        total = term if total is None else total + term
    result[pl.ds(0, rows), :] = total * coarse_scale
    result[pl.ds(rows, wide - rows), :] = jnp.zeros((wide - rows, parents), f32)
    part = wide // 2
    keep[...] = result[pl.ds(pl.multiple_of(c * part, part), part), :]
    send[...] = result[pl.ds(pl.multiple_of((1 - c) * part, part), part), :].astype(bf16)


def coarse_partial(sc, lists, far, own, a, b, own_o, ab_o):
    args = (lists, far, own, a, b, own_o, ab_o)
    shape = (wide // 2, parents)
    return call(
        coarse_kernel,
        sc,
        args,
        [whole(x) for x in args],
        [whole(), whole()],
        [jax.ShapeDtypeStruct(shape, bf16), jax.ShapeDtypeStruct(shape, f32)],
        8,
        scratch=[pltpu.VMEM((rows, 3 * parents), f32), pltpu.VMEM((wide, parents), f32)],
    )


def down_kernel(sc, ops, mine, other, o_ref, op_planes, check, turned_rows):
    c, part = sc[0], wide // 2
    to_planes(ops, op_planes, 8 * share)
    check[pl.ds(pl.multiple_of(c * part, part), part), :] = mine[...]
    check[pl.ds(pl.multiple_of((1 - c) * part, part), part), :] = other[...]
    whole_check = check[...]
    for child in range(8):
        left = every_eighth(op_planes, 8 * share, child, share)
        z = jnp.dot(left, whole_check, preferred_element_type=f32)
        z = jnp.concatenate([z, jnp.zeros((256 - share, parents), f32)], 0).T
        for t in (0, 1):
            turned_rows[pl.ds(t * boxes + child, parents, stride=8), :] = z[
                :, t * 128 : (t + 1) * 128
            ]
    o_ref[pl.ds(0, 128), :] = turned_rows[pl.ds(0, boxes), :].T
    o_ref[pl.ds(128, share - 128), :] = turned_rows[pl.ds(boxes, boxes), :].T[: share - 128]


def downward(sc, ops, mine, other):
    args = (ops, mine, other)
    return call(
        down_kernel,
        sc,
        args,
        [whole(x) for x in args],
        whole(),
        jax.ShapeDtypeStruct((share, boxes), f32),
        12,
        scratch=[
            pltpu.VMEM((tiles * 8 * share, 128), f32),
            pltpu.VMEM((wide, parents), bf16),
            pltpu.VMEM((2 * boxes, 128), f32),
        ],
    )


pitch, step_boxes, unroll = early + 8, 512, 32


def gather_kernel(spots, *refs):
    pieces, o_ref, planes, got = refs[:-3], refs[-3], refs[-2], refs[-1]
    step = pl.program_id(0)
    depth = step_boxes + 8

    @pl.when(step == 0)
    def _():
        at = 0
        for piece in pieces:
            count = piece.shape[0]
            for s in range(tiles):
                planes[pl.ds(s * pitch + at, count), :] = piece[
                    :, s * 128 : (s + 1) * 128
                ].astype(f32)
            at += count
        for s in range(tiles):
            planes[pl.ds(s * pitch + early, 8), :] = jnp.zeros((8, 128), f32)

    def body(i, carry):
        found = [
            planes[pl.ds(spots[step * step_boxes + i * unroll + u], 8, stride=pitch), :]
            for u in range(unroll)
        ]
        for u in range(unroll):
            got[pl.ds(i * unroll + u, 8, stride=depth), :] = found[u]
        return carry

    lax.fori_loop(0, step_boxes // unroll, body, 0)
    for s in range(tiles):
        spot = pl.ds(pl.multiple_of(step * step_boxes, step_boxes), step_boxes)
        o_ref[spot, s * 128 : (s + 1) * 128] = got[pl.ds(s * depth, step_boxes), :].astype(bf16)


def gathered(spots, pieces):
    return call(
        gather_kernel,
        spots,
        tuple(pieces),
        [whole(p) for p in pieces],
        whole(),
        jax.ShapeDtypeStruct((3 * boxes, wide), bf16),
        16,
        grid=(3 * boxes // step_boxes,),
        scratch=[
            pltpu.VMEM((8 * pitch, 128), f32),
            pltpu.VMEM((8 * (step_boxes + 8), 128), f32),
        ],
    )


def far_kernel(start, sc, far, sources, lists, late, late_o, send, keep, result):
    c = sc[0]
    count, most = send.shape[2], result.shape[1]
    late_boxes = jnp.concatenate([late[...], late_o[...]], 0)

    def tile(at, width):
        spot = lax.broadcasted_iota(jnp.int32, (width, 128), 1).astype(f32)
        total = None
        for k in range(3):
            listed = lists[k : k + 1, start + at : start + at + width].astype(f32)
            wanted = jnp.broadcast_to(listed, (128, width)).T
            hot = jnp.concatenate(
                [
                    (wanted == spot + float(base)).astype(f32).astype(bf16)
                    for base in range(0, 2 * chunk, 128)
                ],
                1,
            )
            found = jnp.dot(hot, late_boxes, preferred_element_type=f32)
            found = found + sources[pl.ds(k * boxes + start + at, width), :].astype(f32)
            term = lax.dot_general(
                far[k],
                found.astype(bf16)[:, :rows],
                (((1,), (1,)), ((), ())),
                preferred_element_type=f32,
            )
            total = term if total is None else total + term
        result[:, :width] = total
        lanes = slice(at, at + width)
        for x in (0, 1):
            first = result[pl.ds(share * 2 * x, share), :width]
            second = result[pl.ds(share * (2 * x + 1), share), :width]
            keep[x, :, lanes] = jnp.where(c == 0, first, second)
            send[x, :, lanes] = jnp.where(c == 0, second, first).astype(bf16)

    for at in range(0, count, most):
        tile(at, min(most, count - at))


def far_partial(sc, far, sources, lists, late, late_o, start, count):
    shape = (2, share, count)
    args = (far, sources, lists, late, late_o)
    return call(
        functools.partial(far_kernel, start),
        sc,
        args,
        [whole(x) for x in args],
        [whole(), whole()],
        [jax.ShapeDtypeStruct(shape, bf16), jax.ShapeDtypeStruct(shape, f32)],
        12,
        scratch=[pltpu.VMEM((rows, 256), f32)],
    )


def after(x, *others):
    return lax.optimization_barrier((x, *others))[0]


def local(leaf_density, upward_ops, far_ops, downward_ops, fine_lists, coarse_lists):
    groups = lax.axis_size("space")
    group, rep = lax.axis_index("space"), lax.axis_index("rep")
    l, c = rep >> 1, rep & 1
    no_previous, no_next = group == 0, group == groups - 1
    nowhere = -16384
    base_previous = jnp.where(no_previous, nowhere, 0)
    base_next = jnp.where(no_next, nowhere, 2 * parents)
    sc = jnp.stack(
        [
            c,
            l,
            jnp.where(l == 0, base_previous, base_next),
            jnp.where(l == 0, base_next, base_previous),
        ]
    ).astype(jnp.int32)
    hop = functools.partial(lax.ppermute, axis_name=both, perm=one_hop(groups))
    zswap = functools.partial(lax.ppermute, axis_name=both, perm=across(groups, 2))
    cswap = functools.partial(lax.ppermute, axis_name=both, perm=across(groups, 1))

    def at(i):
        return jnp.reshape(i, (1,)).astype(jnp.int32)

    up_ops = jnp.transpose(upward_ops, (1, 0, 2)).reshape(8 * share, rows)
    down_ops = jnp.transpose(downward_ops, (1, 0, 2)).reshape(8 * share, rows)

    which, side, offset = fine_lists >> 10, (fine_lists >> 9) & 1, fine_lists & (half - 1)
    outside = ((which == 0) & no_previous) | ((which == 2) & no_next)
    direct = (which == 0) == (l == 0)
    theirs = (side != c).astype(jnp.int32)
    is_late = (which != 1) & ~direct & (offset >= half - chunk)
    spots = jnp.where(
        which == 1,
        theirs * half + offset,
        jnp.where(
            direct,
            2 * half + theirs * half + offset,
            4 * half + theirs * (half - chunk) + offset,
        ),
    )
    spots = jnp.where(outside | is_late, early, spots).reshape(-1)
    late_lists = jnp.where(is_late & ~outside, theirs * chunk + offset - (half - chunk), -1)

    head = turned(leaf_density, at(c * half), [chunk])[0]
    rest = jnp.stack([c * half + chunk, (1 - c) * half]).astype(jnp.int32)
    tail, other = turned(leaf_density, after(rest, head), [half - chunk, half])
    up = parent_rows(after(sc, spots, late_lists), up_ops, [head, tail], other)
    own = joined(sc, up, zswap(up))
    ca = hop(own)
    own_o = cswap(own)
    mine = [head, after(tail, own_o)]
    a = [hop(m) for m in mine]
    early_a = after(a[0], ca)
    b = [zswap(early_a)]
    a_o = [cswap(early_a)]
    cb = zswap(ca)
    cab_o = cswap(joined(sc, ca, cb))
    second = after(a[1], early_a, cb, own_o)
    b.append(zswap(second))
    a_o.append(cswap(second))
    b_o = [cswap(b[0])]

    send, keep = coarse_partial(sc, coarse_lists, far_ops, own, ca, cb, own_o, cab_o)
    picked = gathered(after(spots, keep), [*mine, other, *a, *a_o, b[0], b_o[0]])
    shape = (wide // 2, parents)
    part, part_sent = small(add_kernel, sc, (keep, cswap(send)), [(shape, f32), (shape, bf16)])
    b_o.append(cswap(after(b[1], picked, part)))
    part_got = zswap(part_sent)

    def summed(send, keep):
        shape = (share, send.shape[2])
        here, away = small(split_kernel, sc, (keep, cswap(send)), [(shape, f32), (shape, bf16)])
        return here, zswap(away), away

    late = (b[1], b_o[1])
    send, keep = far_partial(after(sc, part), far_ops, picked, late_lists, *late, 0, ahead)
    left = summed(after(send, part_got), keep)
    check = small(add_kernel, sc, (part, part_got), [(shape, bf16)])[0]
    check_o = cswap(check)
    send, keep = far_partial(
        after(sc, check, left[2]), far_ops, picked, late_lists, *late, ahead, boxes - ahead
    )
    right = summed(after(send, left[1], check_o), keep)
    spread = downward(after(sc, right[2]), down_ops, check, check_o)
    return small(last_kernel, sc, (spread, *left[:2], *right[:2]), [((share, boxes), bf16)])[0]


def solution(mesh):
    return jax.shard_map(
        local,
        mesh=mesh,
        in_specs=(
            P(None, "space"),
            P(None, "rep", None),
            P("rep", None, None),
            P(None, "rep", None),
            P("rep", "space"),
            P("rep", "space"),
        ),
        out_specs=P("rep", "space"),
        check_vma=False,
    )
```

```python
import functools

import jax
import jax.numpy as jnp
from jax import lax
from jax.experimental import pallas as pl
from jax.experimental.pallas import tpu as pltpu
from jax.sharding import PartitionSpec as P

bf16, f32 = jnp.bfloat16, jnp.float32
both = ("space", "rep")
coarse_scale = 0.5
rows, wide, tiles = 888, 896, 7
boxes, half = 1024, 512
parents = 128
share = 222
chunks = 2
chunk = half // chunks
early = 6 * half - 2 * chunk
ahead = 512


def one_hop(groups):
    up = [(4 * s + 2 + c, 4 * (s + 1) + c) for s in range(groups - 1) for c in (0, 1)]
    up += [(0, 1), (4 * groups - 2, 4 * groups - 1)]
    return up + [(j, i) for i, j in up]


def across(groups, flip):
    return [(4 * s + r, 4 * s + (r ^ flip)) for s in range(groups) for r in range(4)]


def call(kernel, scalars, args, in_specs, out_specs, out_shape, limit, grid=(1,), scratch=()):
    return pl.pallas_call(
        kernel,
        grid_spec=pltpu.PrefetchScalarGridSpec(
            num_scalar_prefetch=1,
            grid=grid,
            in_specs=in_specs,
            out_specs=out_specs,
            scratch_shapes=scratch,
        ),
        out_shape=out_shape,
        compiler_params=pltpu.CompilerParams(vmem_limit_bytes=limit << 20),
        cost_estimate=pl.CostEstimate(flops=0, bytes_accessed=0, transcendentals=0),
    )(scalars, *args)


def whole(a=None):
    return pl.BlockSpec(memory_space=pltpu.VMEM)


def turn_kernel(firsts, x_ref, *outs):
    for n, o_ref in enumerate(outs):
        for i in range(o_ref.shape[0] // 128):
            part = x_ref[:, pl.ds(pl.multiple_of(firsts[n] + i * 128, 128), 128)].astype(f32)
            tall = jnp.concatenate([part, jnp.zeros((wide - rows, 128), f32)], 0)
            o_ref[pl.ds(i * 128, 128), :] = tall.T.astype(bf16)


def turned(x, firsts, counts):
    shapes = [jax.ShapeDtypeStruct((n, wide), bf16) for n in counts]
    return call(turn_kernel, firsts, (x,), [whole()], [whole() for _ in counts], shapes, 8)


def small(kernel, sc, args, shapes, limit=6):
    shapes = [jax.ShapeDtypeStruct(*s) for s in shapes]
    return call(kernel, sc, args, [whole() for _ in args], [whole() for _ in shapes], shapes, limit)


def join_kernel(sc, *refs):
    at = 0
    for part in refs[:-1]:
        refs[-1][:, at : at + part.shape[1]] = part[...]
        at += part.shape[1]


def joined(sc, *parts):
    width = sum(p.shape[1] for p in parts)
    return small(join_kernel, sc, parts, [((parts[0].shape[0], width), bf16)])[0]


def split_kernel(sc, keep, got, here, away):
    l = sc[1]
    here[...] = keep[l] + got[l].astype(f32)
    away[...] = (keep[1 - l] + got[1 - l].astype(f32)).astype(bf16)


def add_kernel(sc, one, two, *outs):
    total = one[...] + two[...].astype(f32)
    for o_ref in outs:
        o_ref[...] = total.astype(o_ref.dtype)


def last_kernel(sc, spread, *refs):
    o_ref, at = refs[-1], 0
    for here, there in zip(refs[:-1:2], refs[1:-1:2]):
        lanes = slice(at, at + here.shape[1])
        o_ref[:, lanes] = (here[...] + there[...].astype(f32) + spread[:, lanes]).astype(bf16)
        at += here.shape[1]


def to_planes(src, dst, height):
    for s in range(tiles - 1):
        dst[pl.ds(s * height, height), :] = src[:, s * 128 : (s + 1) * 128].astype(f32)
    last = src[:, (tiles - 1) * 128 :].astype(f32)
    if last.shape[1] < 128:
        last = jnp.concatenate([last, jnp.zeros((height, 128 - last.shape[1]), f32)], 1)
    dst[pl.ds((tiles - 1) * height, height), :] = last


def every_eighth(planes, height, child, count):
    parts = [planes[pl.ds(s * height + child, count, stride=8), :] for s in range(tiles)]
    return jnp.concatenate(parts, 1).astype(bf16)


def up_kernel(sc, ops, other, *refs):
    mine, o_ref, op_planes, box_planes = refs[:-3], refs[-3], refs[-2], refs[-1]
    to_planes(ops, op_planes, 8 * share)
    for s in range(tiles):
        lanes = slice(s * 128, (s + 1) * 128)
        for i, part in enumerate(mine):
            at = pl.multiple_of(s * boxes + sc[0] * half + i * chunk, chunk)
            box_planes[pl.ds(at, chunk), :] = part[:, lanes].astype(f32)
        at = pl.multiple_of(s * boxes + (1 - sc[0]) * half, half)
        box_planes[pl.ds(at, half), :] = other[:, lanes].astype(f32)
    total = None
    for child in range(8):
        left = every_eighth(op_planes, 8 * share, child, share)
        right = every_eighth(box_planes, boxes, child, parents)
        term = lax.dot_general(left, right, (((1,), (1,)), ((), ())), preferred_element_type=f32)
        total = term if total is None else total + term
    o_ref[...] = total.astype(bf16)


def parent_rows(sc, ops, mine, other):
    args = (ops, other, *mine)
    return call(
        up_kernel,
        sc,
        args,
        [whole(a) for a in args],
        whole(),
        jax.ShapeDtypeStruct((share, parents), bf16),
        14,
        scratch=[
            pltpu.VMEM((tiles * 8 * share, 128), f32),
            pltpu.VMEM((tiles * boxes, 128), f32),
        ],
    )


def coarse_kernel(sc, lists, far, own, a, b, own_o, a_o, b_o, send, keep, picked, result):
    c, l = sc[0], sc[1]
    wanted = jnp.concatenate([lists[k : k + 1, :] for k in range(3)], 1)
    count = wanted.shape[1]
    spot = lax.broadcasted_iota(jnp.int32, (parents, count), 0)
    hot = jnp.concatenate(
        [
            (spot == wanted - base).astype(f32).astype(bf16)
            for base in (parents, sc[2], sc[3])
        ],
        0,
    )

    def pick(*parts):
        return jnp.dot(jnp.concatenate(parts, 1), hot, preferred_element_type=f32)

    lo, hi = slice(0, parents), slice(parents, 2 * parents)
    found = (
        (pick(own[:, lo], a[:, hi], b[:, lo]), pick(own[:, hi], a[:, lo], b[:, hi])),
        (pick(own_o[:, lo], a_o[:, hi], b_o[:, lo]), pick(own_o[:, hi], a_o[:, lo], b_o[:, hi])),
    )
    for j in range(4):
        x, y = j // 2, j % 2
        mine = jnp.where(l == x, found[0][0], found[0][1])
        theirs = jnp.where(l == x, found[1][0], found[1][1])
        picked[pl.ds(share * j, share), :] = jnp.where(c == y, mine, theirs)
    sources = picked[...].astype(bf16)
    total = None
    for k in range(3):
        term = jnp.dot(
            far[k], sources[:, k * parents : (k + 1) * parents], preferred_element_type=f32
        )
        total = term if total is None else total + term
    result[pl.ds(0, rows), :] = total * coarse_scale
    result[pl.ds(rows, wide - rows), :] = jnp.zeros((wide - rows, parents), f32)
    part = wide // 2
    keep[...] = result[pl.ds(pl.multiple_of(c * part, part), part), :]
    send[...] = result[pl.ds(pl.multiple_of((1 - c) * part, part), part), :].astype(bf16)


def coarse_partial(sc, lists, far, own, a, b, own_o, a_o, b_o):
    args = (lists, far, own, a, b, own_o, a_o, b_o)
    shape = (wide // 2, parents)
    return call(
        coarse_kernel,
        sc,
        args,
        [whole(x) for x in args],
        [whole(), whole()],
        [jax.ShapeDtypeStruct(shape, bf16), jax.ShapeDtypeStruct(shape, f32)],
        8,
        scratch=[pltpu.VMEM((rows, 3 * parents), f32), pltpu.VMEM((wide, parents), f32)],
    )


def down_kernel(sc, ops, mine, other, o_ref, op_planes, check, turned_rows):
    c, part = sc[0], wide // 2
    to_planes(ops, op_planes, 8 * share)
    check[pl.ds(pl.multiple_of(c * part, part), part), :] = mine[...]
    check[pl.ds(pl.multiple_of((1 - c) * part, part), part), :] = other[...]
    whole_check = check[...]
    for child in range(8):
        left = every_eighth(op_planes, 8 * share, child, share)
        z = jnp.dot(left, whole_check, preferred_element_type=f32)
        z = jnp.concatenate([z, jnp.zeros((256 - share, parents), f32)], 0).T
        for t in (0, 1):
            turned_rows[pl.ds(t * boxes + child, parents, stride=8), :] = z[
                :, t * 128 : (t + 1) * 128
            ]
    o_ref[pl.ds(0, 128), :] = turned_rows[pl.ds(0, boxes), :].T
    o_ref[pl.ds(128, share - 128), :] = turned_rows[pl.ds(boxes, boxes), :].T[: share - 128]


def downward(sc, ops, mine, other):
    args = (ops, mine, other)
    return call(
        down_kernel,
        sc,
        args,
        [whole(x) for x in args],
        whole(),
        jax.ShapeDtypeStruct((share, boxes), f32),
        12,
        scratch=[
            pltpu.VMEM((tiles * 8 * share, 128), f32),
            pltpu.VMEM((wide, parents), bf16),
            pltpu.VMEM((2 * boxes, 128), f32),
        ],
    )


pitch, step_boxes, unroll = early + 8, 512, 32


def gather_kernel(spots, *refs):
    pieces, o_ref, planes, got = refs[:-3], refs[-3], refs[-2], refs[-1]
    step = pl.program_id(0)
    depth = step_boxes + 8

    @pl.when(step == 0)
    def _():
        at = 0
        for piece in pieces:
            count = piece.shape[0]
            for s in range(tiles):
                planes[pl.ds(s * pitch + at, count), :] = piece[
                    :, s * 128 : (s + 1) * 128
                ].astype(f32)
            at += count
        for s in range(tiles):
            planes[pl.ds(s * pitch + early, 8), :] = jnp.zeros((8, 128), f32)

    def body(i, carry):
        found = [
            planes[pl.ds(spots[step * step_boxes + i * unroll + u], 8, stride=pitch), :]
            for u in range(unroll)
        ]
        for u in range(unroll):
            got[pl.ds(i * unroll + u, 8, stride=depth), :] = found[u]
        return carry

    lax.fori_loop(0, step_boxes // unroll, body, 0)
    for s in range(tiles):
        spot = pl.ds(pl.multiple_of(step * step_boxes, step_boxes), step_boxes)
        o_ref[spot, s * 128 : (s + 1) * 128] = got[pl.ds(s * depth, step_boxes), :].astype(bf16)


def gathered(spots, pieces):
    return call(
        gather_kernel,
        spots,
        tuple(pieces),
        [whole(p) for p in pieces],
        whole(),
        jax.ShapeDtypeStruct((3 * boxes, wide), bf16),
        16,
        grid=(3 * boxes // step_boxes,),
        scratch=[
            pltpu.VMEM((8 * pitch, 128), f32),
            pltpu.VMEM((8 * (step_boxes + 8), 128), f32),
        ],
    )


def far_kernel(start, sc, far, sources, lists, late, late_o, send, keep, result):
    c = sc[0]
    count, most = send.shape[2], result.shape[1]
    late_boxes = jnp.concatenate([late[...], late_o[...]], 0)

    def tile(at, width):
        spot = lax.broadcasted_iota(jnp.int32, (width, 128), 1).astype(f32)
        total = None
        for k in range(3):
            listed = lists[k : k + 1, start + at : start + at + width].astype(f32)
            wanted = jnp.broadcast_to(listed, (128, width)).T
            hot = jnp.concatenate(
                [
                    (wanted == spot + float(base)).astype(f32).astype(bf16)
                    for base in range(0, 2 * chunk, 128)
                ],
                1,
            )
            found = jnp.dot(hot, late_boxes, preferred_element_type=f32)
            found = found + sources[pl.ds(k * boxes + start + at, width), :].astype(f32)
            term = lax.dot_general(
                far[k],
                found.astype(bf16)[:, :rows],
                (((1,), (1,)), ((), ())),
                preferred_element_type=f32,
            )
            total = term if total is None else total + term
        result[:, :width] = total
        lanes = slice(at, at + width)
        for x in (0, 1):
            first = result[pl.ds(share * 2 * x, share), :width]
            second = result[pl.ds(share * (2 * x + 1), share), :width]
            keep[x, :, lanes] = jnp.where(c == 0, first, second)
            send[x, :, lanes] = jnp.where(c == 0, second, first).astype(bf16)

    for at in range(0, count, most):
        tile(at, min(most, count - at))


def far_partial(sc, far, sources, lists, late, late_o, start, count):
    shape = (2, share, count)
    args = (far, sources, lists, late, late_o)
    return call(
        functools.partial(far_kernel, start),
        sc,
        args,
        [whole(x) for x in args],
        [whole(), whole()],
        [jax.ShapeDtypeStruct(shape, bf16), jax.ShapeDtypeStruct(shape, f32)],
        12,
        scratch=[pltpu.VMEM((rows, 256), f32)],
    )


def after(x, *others):
    return lax.optimization_barrier((x, *others))[0]


def local(leaf_density, upward_ops, far_ops, downward_ops, fine_lists, coarse_lists):
    groups = lax.axis_size("space")
    group, rep = lax.axis_index("space"), lax.axis_index("rep")
    l, c = rep >> 1, rep & 1
    no_previous, no_next = group == 0, group == groups - 1
    nowhere = -16384
    base_previous = jnp.where(no_previous, nowhere, 0)
    base_next = jnp.where(no_next, nowhere, 2 * parents)
    sc = jnp.stack(
        [
            c,
            l,
            jnp.where(l == 0, base_previous, base_next),
            jnp.where(l == 0, base_next, base_previous),
        ]
    ).astype(jnp.int32)
    hop = functools.partial(lax.ppermute, axis_name=both, perm=one_hop(groups))
    zswap = functools.partial(lax.ppermute, axis_name=both, perm=across(groups, 2))
    cswap = functools.partial(lax.ppermute, axis_name=both, perm=across(groups, 1))

    def at(i):
        return jnp.reshape(i, (1,)).astype(jnp.int32)

    up_ops = jnp.transpose(upward_ops, (1, 0, 2)).reshape(8 * share, rows)
    down_ops = jnp.transpose(downward_ops, (1, 0, 2)).reshape(8 * share, rows)

    which, side, offset = fine_lists >> 10, (fine_lists >> 9) & 1, fine_lists & (half - 1)
    outside = ((which == 0) & no_previous) | ((which == 2) & no_next)
    direct = (which == 0) == (l == 0)
    theirs = (side != c).astype(jnp.int32)
    is_late = (which != 1) & ~direct & (offset >= half - chunk)
    spots = jnp.where(
        which == 1,
        theirs * half + offset,
        jnp.where(
            direct,
            2 * half + theirs * half + offset,
            4 * half + theirs * (half - chunk) + offset,
        ),
    )
    spots = jnp.where(outside | is_late, early, spots).reshape(-1)
    late_lists = jnp.where(is_late & ~outside, theirs * chunk + offset - (half - chunk), -1)

    head = turned(leaf_density, at(c * half), [chunk])[0]
    rest = jnp.stack([c * half + chunk, (1 - c) * half]).astype(jnp.int32)
    tail, other = turned(leaf_density, after(rest, head), [half - chunk, half])
    up = parent_rows(after(sc, spots, late_lists), up_ops, [head, tail], other)
    own = joined(sc, up, zswap(up))
    ca = hop(own)
    own_o = cswap(own)
    mine = [head, after(tail, up)]
    a = [hop(m) for m in mine]
    early_a = after(a[0], own)
    second = after(a[1], early_a, own_o)
    b = [zswap(early_a), zswap(second)]
    a_o = [cswap(early_a), cswap(after(second, ca))]
    cb, ca_o = zswap(ca), cswap(ca)
    b_o = [cswap(b[0])]
    picked = gathered(spots, [*mine, other, *a, *a_o, b[0], b_o[0]])
    b_o.append(cswap(after(b[1], picked, cb)))
    cb_o = cswap(cb)

    def summed(send, keep):
        shape = (share, send.shape[2])
        here, away = small(split_kernel, sc, (keep, cswap(send)), [(shape, f32), (shape, bf16)])
        return here, zswap(away), away

    late = (b[1], b_o[1])
    send, keep = far_partial(sc, far_ops, picked, late_lists, *late, 0, ahead)
    left = summed(after(send, cb_o, ca_o), keep)
    send, keep = coarse_partial(
        after(sc, send), coarse_lists, far_ops, own, ca, cb, own_o, ca_o, cb_o
    )
    shape = (wide // 2, parents)
    part, part_sent = small(
        add_kernel, after(sc, left[2]), (keep, cswap(send)), [(shape, f32), (shape, bf16)]
    )
    send, keep = far_partial(
        after(sc, part), far_ops, picked, late_lists, *late, ahead, boxes - ahead
    )
    part_got = zswap(part_sent)
    right = summed(after(send, left[1], part_got), keep)
    check = small(add_kernel, sc, (part, part_got), [(shape, bf16)])[0]
    check_o = cswap(check)
    spread = downward(after(sc, right[2]), down_ops, check, check_o)
    return small(last_kernel, sc, (spread, *left[:2], *right[:2]), [((share, boxes), bf16)])[0]


def solution(mesh):
    return jax.shard_map(
        local,
        mesh=mesh,
        in_specs=(
            P(None, "space"),
            P(None, "rep", None),
            P("rep", None, None),
            P(None, "rep", None),
            P("rep", "space"),
            P("rep", "space"),
        ),
        out_specs=P("rep", "space"),
        check_vma=False,
    )
```

```python
import functools

import jax
import jax.numpy as jnp
from jax import lax
from jax.experimental import pallas as pl
from jax.experimental.pallas import tpu as pltpu
from jax.sharding import PartitionSpec as P

bf16, f32 = jnp.bfloat16, jnp.float32
both = ("space", "rep")
coarse_scale = 0.5
rows, wide, tiles = 888, 896, 7
boxes, half = 1024, 512
parents = 128
share = 222
chunks = 2
chunk = half // chunks
early = 6 * half - 2 * chunk
ahead = 512


def one_hop(groups):
    up = [(4 * s + 2 + c, 4 * (s + 1) + c) for s in range(groups - 1) for c in (0, 1)]
    up += [(0, 1), (4 * groups - 2, 4 * groups - 1)]
    return up + [(j, i) for i, j in up]


def across(groups, flip):
    return [(4 * s + r, 4 * s + (r ^ flip)) for s in range(groups) for r in range(4)]


def call(kernel, scalars, args, in_specs, out_specs, out_shape, limit, grid=(1,), scratch=()):
    return pl.pallas_call(
        kernel,
        grid_spec=pltpu.PrefetchScalarGridSpec(
            num_scalar_prefetch=1,
            grid=grid,
            in_specs=in_specs,
            out_specs=out_specs,
            scratch_shapes=scratch,
        ),
        out_shape=out_shape,
        compiler_params=pltpu.CompilerParams(vmem_limit_bytes=limit << 20),
        cost_estimate=pl.CostEstimate(flops=0, bytes_accessed=0, transcendentals=0),
    )(scalars, *args)


def whole(a=None):
    return pl.BlockSpec(memory_space=pltpu.VMEM)


def turn_kernel(firsts, x_ref, *outs):
    for n, o_ref in enumerate(outs):
        for i in range(o_ref.shape[0] // 128):
            part = x_ref[:, pl.ds(pl.multiple_of(firsts[n] + i * 128, 128), 128)].astype(f32)
            tall = jnp.concatenate([part, jnp.zeros((wide - rows, 128), f32)], 0)
            o_ref[pl.ds(i * 128, 128), :] = tall.T.astype(bf16)


def turned(x, firsts, counts):
    shapes = [jax.ShapeDtypeStruct((n, wide), bf16) for n in counts]
    return call(turn_kernel, firsts, (x,), [whole()], [whole() for _ in counts], shapes, 8)


def small(kernel, sc, args, shapes, limit=6):
    shapes = [jax.ShapeDtypeStruct(*s) for s in shapes]
    return call(kernel, sc, args, [whole() for _ in args], [whole() for _ in shapes], shapes, limit)


def join_kernel(sc, *refs):
    at = 0
    for part in refs[:-1]:
        refs[-1][:, at : at + part.shape[1]] = part[...]
        at += part.shape[1]


def joined(sc, *parts):
    width = sum(p.shape[1] for p in parts)
    return small(join_kernel, sc, parts, [((parts[0].shape[0], width), bf16)])[0]


def split_kernel(sc, keep, got, here, away):
    l = sc[1]
    here[...] = keep[l] + got[l].astype(f32)
    away[...] = (keep[1 - l] + got[1 - l].astype(f32)).astype(bf16)


def add_kernel(sc, one, two, *outs):
    total = one[...] + two[...].astype(f32)
    for o_ref in outs:
        o_ref[...] = total.astype(o_ref.dtype)


def last_kernel(sc, spread, *refs):
    o_ref, at = refs[-1], 0
    for here, there in zip(refs[:-1:2], refs[1:-1:2]):
        lanes = slice(at, at + here.shape[1])
        o_ref[:, lanes] = (here[...] + there[...].astype(f32) + spread[:, lanes]).astype(bf16)
        at += here.shape[1]


def to_planes(src, dst, height):
    for s in range(tiles - 1):
        dst[pl.ds(s * height, height), :] = src[:, s * 128 : (s + 1) * 128].astype(f32)
    last = src[:, (tiles - 1) * 128 :].astype(f32)
    if last.shape[1] < 128:
        last = jnp.concatenate([last, jnp.zeros((height, 128 - last.shape[1]), f32)], 1)
    dst[pl.ds((tiles - 1) * height, height), :] = last


def every_eighth(planes, height, child, count):
    parts = [planes[pl.ds(s * height + child, count, stride=8), :] for s in range(tiles)]
    return jnp.concatenate(parts, 1).astype(bf16)


def up_kernel(sc, ops, other, *refs):
    mine, o_ref, op_planes, box_planes = refs[:-3], refs[-3], refs[-2], refs[-1]
    to_planes(ops, op_planes, 8 * share)
    for s in range(tiles):
        lanes = slice(s * 128, (s + 1) * 128)
        for i, part in enumerate(mine):
            at = pl.multiple_of(s * boxes + sc[0] * half + i * chunk, chunk)
            box_planes[pl.ds(at, chunk), :] = part[:, lanes].astype(f32)
        at = pl.multiple_of(s * boxes + (1 - sc[0]) * half, half)
        box_planes[pl.ds(at, half), :] = other[:, lanes].astype(f32)
    total = None
    for child in range(8):
        left = every_eighth(op_planes, 8 * share, child, share)
        right = every_eighth(box_planes, boxes, child, parents)
        term = lax.dot_general(left, right, (((1,), (1,)), ((), ())), preferred_element_type=f32)
        total = term if total is None else total + term
    o_ref[...] = total.astype(bf16)


def parent_rows(sc, ops, mine, other):
    args = (ops, other, *mine)
    return call(
        up_kernel,
        sc,
        args,
        [whole(a) for a in args],
        whole(),
        jax.ShapeDtypeStruct((share, parents), bf16),
        14,
        scratch=[
            pltpu.VMEM((tiles * 8 * share, 128), f32),
            pltpu.VMEM((tiles * boxes, 128), f32),
        ],
    )


def coarse_kernel(sc, lists, far, own, a, b, own_o, a_o, b_o, send, keep, picked, result):
    c, l = sc[0], sc[1]
    wanted = jnp.concatenate([lists[k : k + 1, :] for k in range(3)], 1)
    count = wanted.shape[1]
    spot = lax.broadcasted_iota(jnp.int32, (parents, count), 0)
    hot = jnp.concatenate(
        [
            (spot == wanted - base).astype(f32).astype(bf16)
            for base in (parents, sc[2], sc[3])
        ],
        0,
    )

    def pick(*parts):
        return jnp.dot(jnp.concatenate(parts, 1), hot, preferred_element_type=f32)

    lo, hi = slice(0, parents), slice(parents, 2 * parents)
    found = (
        (pick(own[:, lo], a[:, hi], b[:, lo]), pick(own[:, hi], a[:, lo], b[:, hi])),
        (pick(own_o[:, lo], a_o[:, hi], b_o[:, lo]), pick(own_o[:, hi], a_o[:, lo], b_o[:, hi])),
    )
    for j in range(4):
        x, y = j // 2, j % 2
        mine = jnp.where(l == x, found[0][0], found[0][1])
        theirs = jnp.where(l == x, found[1][0], found[1][1])
        picked[pl.ds(share * j, share), :] = jnp.where(c == y, mine, theirs)
    sources = picked[...].astype(bf16)
    total = None
    for k in range(3):
        term = jnp.dot(
            far[k], sources[:, k * parents : (k + 1) * parents], preferred_element_type=f32
        )
        total = term if total is None else total + term
    result[pl.ds(0, rows), :] = total * coarse_scale
    result[pl.ds(rows, wide - rows), :] = jnp.zeros((wide - rows, parents), f32)
    part = wide // 2
    keep[...] = result[pl.ds(pl.multiple_of(c * part, part), part), :]
    send[...] = result[pl.ds(pl.multiple_of((1 - c) * part, part), part), :].astype(bf16)


def coarse_partial(sc, lists, far, own, a, b, own_o, a_o, b_o):
    args = (lists, far, own, a, b, own_o, a_o, b_o)
    shape = (wide // 2, parents)
    return call(
        coarse_kernel,
        sc,
        args,
        [whole(x) for x in args],
        [whole(), whole()],
        [jax.ShapeDtypeStruct(shape, bf16), jax.ShapeDtypeStruct(shape, f32)],
        8,
        scratch=[pltpu.VMEM((rows, 3 * parents), f32), pltpu.VMEM((wide, parents), f32)],
    )


def down_kernel(sc, ops, mine, other, o_ref, op_planes, check, turned_rows):
    c, part = sc[0], wide // 2
    to_planes(ops, op_planes, 8 * share)
    check[pl.ds(pl.multiple_of(c * part, part), part), :] = mine[...]
    check[pl.ds(pl.multiple_of((1 - c) * part, part), part), :] = other[...]
    whole_check = check[...]
    for child in range(8):
        left = every_eighth(op_planes, 8 * share, child, share)
        z = jnp.dot(left, whole_check, preferred_element_type=f32)
        z = jnp.concatenate([z, jnp.zeros((256 - share, parents), f32)], 0).T
        for t in (0, 1):
            turned_rows[pl.ds(t * boxes + child, parents, stride=8), :] = z[
                :, t * 128 : (t + 1) * 128
            ]
    o_ref[pl.ds(0, 128), :] = turned_rows[pl.ds(0, boxes), :].T
    o_ref[pl.ds(128, share - 128), :] = turned_rows[pl.ds(boxes, boxes), :].T[: share - 128]


def downward(sc, ops, mine, other):
    args = (ops, mine, other)
    return call(
        down_kernel,
        sc,
        args,
        [whole(x) for x in args],
        whole(),
        jax.ShapeDtypeStruct((share, boxes), f32),
        12,
        scratch=[
            pltpu.VMEM((tiles * 8 * share, 128), f32),
            pltpu.VMEM((wide, parents), bf16),
            pltpu.VMEM((2 * boxes, 128), f32),
        ],
    )


pitch, step_boxes, unroll = early + 8, 512, 32


def gather_kernel(spots, *refs):
    pieces, o_ref, planes, got = refs[:-3], refs[-3], refs[-2], refs[-1]
    step = pl.program_id(0)
    depth = step_boxes + 8

    @pl.when(step == 0)
    def _():
        at = 0
        for piece in pieces:
            count = piece.shape[0]
            for s in range(tiles):
                planes[pl.ds(s * pitch + at, count), :] = piece[
                    :, s * 128 : (s + 1) * 128
                ].astype(f32)
            at += count
        for s in range(tiles):
            planes[pl.ds(s * pitch + early, 8), :] = jnp.zeros((8, 128), f32)

    def body(i, carry):
        found = [
            planes[pl.ds(spots[step * step_boxes + i * unroll + u], 8, stride=pitch), :]
            for u in range(unroll)
        ]
        for u in range(unroll):
            got[pl.ds(i * unroll + u, 8, stride=depth), :] = found[u]
        return carry

    lax.fori_loop(0, step_boxes // unroll, body, 0)
    for s in range(tiles):
        spot = pl.ds(pl.multiple_of(step * step_boxes, step_boxes), step_boxes)
        o_ref[spot, s * 128 : (s + 1) * 128] = got[pl.ds(s * depth, step_boxes), :].astype(bf16)


def gathered(spots, pieces):
    return call(
        gather_kernel,
        spots,
        tuple(pieces),
        [whole(p) for p in pieces],
        whole(),
        jax.ShapeDtypeStruct((3 * boxes, wide), bf16),
        16,
        grid=(3 * boxes // step_boxes,),
        scratch=[
            pltpu.VMEM((8 * pitch, 128), f32),
            pltpu.VMEM((8 * (step_boxes + 8), 128), f32),
        ],
    )


def far_kernel(start, sc, far, sources, lists, late, late_o, send, keep, result):
    c = sc[0]
    count, most = send.shape[2], result.shape[1]
    late_boxes = jnp.concatenate([late[...], late_o[...]], 0)

    def tile(at, width):
        spot = lax.broadcasted_iota(jnp.int32, (width, 128), 1).astype(f32)
        total = None
        for k in range(3):
            listed = lists[k : k + 1, start + at : start + at + width].astype(f32)
            wanted = jnp.broadcast_to(listed, (128, width)).T
            hot = jnp.concatenate(
                [
                    (wanted == spot + float(base)).astype(f32).astype(bf16)
                    for base in range(0, 2 * chunk, 128)
                ],
                1,
            )
            found = jnp.dot(hot, late_boxes, preferred_element_type=f32)
            found = found + sources[pl.ds(k * boxes + start + at, width), :].astype(f32)
            term = lax.dot_general(
                far[k],
                found.astype(bf16)[:, :rows],
                (((1,), (1,)), ((), ())),
                preferred_element_type=f32,
            )
            total = term if total is None else total + term
        result[:, :width] = total
        lanes = slice(at, at + width)
        for x in (0, 1):
            first = result[pl.ds(share * 2 * x, share), :width]
            second = result[pl.ds(share * (2 * x + 1), share), :width]
            keep[x, :, lanes] = jnp.where(c == 0, first, second)
            send[x, :, lanes] = jnp.where(c == 0, second, first).astype(bf16)

    for at in range(0, count, most):
        tile(at, min(most, count - at))


def far_partial(sc, far, sources, lists, late, late_o, start, count):
    shape = (2, share, count)
    args = (far, sources, lists, late, late_o)
    return call(
        functools.partial(far_kernel, start),
        sc,
        args,
        [whole(x) for x in args],
        [whole(), whole()],
        [jax.ShapeDtypeStruct(shape, bf16), jax.ShapeDtypeStruct(shape, f32)],
        12,
        scratch=[pltpu.VMEM((rows, 256), f32)],
    )


def after(x, *others):
    return lax.optimization_barrier((x, *others))[0]


def local(leaf_density, upward_ops, far_ops, downward_ops, fine_lists, coarse_lists):
    groups = lax.axis_size("space")
    group, rep = lax.axis_index("space"), lax.axis_index("rep")
    l, c = rep >> 1, rep & 1
    no_previous, no_next = group == 0, group == groups - 1
    nowhere = -16384
    base_previous = jnp.where(no_previous, nowhere, 0)
    base_next = jnp.where(no_next, nowhere, 2 * parents)
    sc = jnp.stack(
        [
            c,
            l,
            jnp.where(l == 0, base_previous, base_next),
            jnp.where(l == 0, base_next, base_previous),
        ]
    ).astype(jnp.int32)
    hop = functools.partial(lax.ppermute, axis_name=both, perm=one_hop(groups))
    zswap = functools.partial(lax.ppermute, axis_name=both, perm=across(groups, 2))
    cswap = functools.partial(lax.ppermute, axis_name=both, perm=across(groups, 1))

    def at(i):
        return jnp.reshape(i, (1,)).astype(jnp.int32)

    up_ops = jnp.transpose(upward_ops, (1, 0, 2)).reshape(8 * share, rows)
    down_ops = jnp.transpose(downward_ops, (1, 0, 2)).reshape(8 * share, rows)

    which, side, offset = fine_lists >> 10, (fine_lists >> 9) & 1, fine_lists & (half - 1)
    outside = ((which == 0) & no_previous) | ((which == 2) & no_next)
    direct = (which == 0) == (l == 0)
    theirs = (side != c).astype(jnp.int32)
    is_late = (which != 1) & ~direct & (offset >= half - chunk)
    spots = jnp.where(
        which == 1,
        theirs * half + offset,
        jnp.where(
            direct,
            2 * half + theirs * half + offset,
            4 * half + theirs * (half - chunk) + offset,
        ),
    )
    spots = jnp.where(outside | is_late, early, spots).reshape(-1)
    late_lists = jnp.where(is_late & ~outside, theirs * chunk + offset - (half - chunk), -1)

    head = turned(leaf_density, at(c * half), [chunk])[0]
    rest = jnp.stack([c * half + chunk, (1 - c) * half]).astype(jnp.int32)
    tail, other = turned(leaf_density, after(rest, head), [half - chunk, half])
    up = parent_rows(after(sc, spots, late_lists), up_ops, [head, tail], other)
    own = joined(sc, up, zswap(up))
    ca = hop(own)
    own_o = cswap(own)
    mine = [head, after(tail, up)]
    a = [hop(m) for m in mine]
    early_a = after(a[0], own)
    cb, ca_o = zswap(ca), cswap(ca)
    second = after(a[1], early_a, own_o, cb)
    b = [zswap(early_a), zswap(second)]
    a_o = [cswap(early_a), cswap(second)]
    cb_o = cswap(cb)
    b_o = [cswap(b[0])]
    picked = gathered(spots, [*mine, other, *a, *a_o, b[0], b_o[0]])

    send, keep = coarse_partial(
        after(sc, picked), coarse_lists, far_ops, own, ca, cb, own_o, ca_o, cb_o
    )
    b_o.append(cswap(after(b[1], keep)))
    shape = (wide // 2, parents)
    part, part_sent = small(add_kernel, sc, (keep, cswap(send)), [(shape, f32), (shape, bf16)])
    part_got = zswap(part_sent)

    def summed(send, keep):
        shape = (share, send.shape[2])
        here, away = small(split_kernel, sc, (keep, cswap(send)), [(shape, f32), (shape, bf16)])
        return here, zswap(away), away

    late = (b[1], b_o[1])
    send, keep = far_partial(after(sc, part), far_ops, picked, late_lists, *late, 0, ahead)
    left = summed(after(send, part_got), keep)
    check = small(add_kernel, sc, (part, part_got), [(shape, bf16)])[0]
    check_o = cswap(check)
    send, keep = far_partial(
        after(sc, check, left[2]), far_ops, picked, late_lists, *late, ahead, boxes - ahead
    )
    right = summed(after(send, left[1], check_o), keep)
    spread = downward(after(sc, right[2]), down_ops, check, check_o)
    return small(last_kernel, sc, (spread, *left[:2], *right[:2]), [((share, boxes), bf16)])[0]


def solution(mesh):
    return jax.shard_map(
        local,
        mesh=mesh,
        in_specs=(
            P(None, "space"),
            P(None, "rep", None),
            P("rep", None, None),
            P(None, "rep", None),
            P("rep", "space"),
            P("rep", "space"),
        ),
        out_specs=P("rep", "space"),
        check_vma=False,
    )
```

```python
import functools

import jax
import jax.numpy as jnp
from jax import lax
from jax.experimental import pallas as pl
from jax.experimental.pallas import tpu as pltpu
from jax.sharding import PartitionSpec as P

bf16, f32 = jnp.bfloat16, jnp.float32
both = ("space", "rep")
coarse_scale = 0.5
rows, wide, tiles = 888, 896, 7
boxes, half = 1024, 512
parents = 128
share = 222
chunks = 4
chunk = half // chunks
early = 6 * half - 2 * chunk
ahead = 640


def one_hop(groups):
    up = [(4 * s + 2 + c, 4 * (s + 1) + c) for s in range(groups - 1) for c in (0, 1)]
    up += [(0, 1), (4 * groups - 2, 4 * groups - 1)]
    return up + [(j, i) for i, j in up]


def across(groups, flip):
    return [(4 * s + r, 4 * s + (r ^ flip)) for s in range(groups) for r in range(4)]


def call(kernel, scalars, args, in_specs, out_specs, out_shape, limit, grid=(1,), scratch=()):
    return pl.pallas_call(
        kernel,
        grid_spec=pltpu.PrefetchScalarGridSpec(
            num_scalar_prefetch=1,
            grid=grid,
            in_specs=in_specs,
            out_specs=out_specs,
            scratch_shapes=scratch,
        ),
        out_shape=out_shape,
        compiler_params=pltpu.CompilerParams(vmem_limit_bytes=limit << 20),
        cost_estimate=pl.CostEstimate(flops=0, bytes_accessed=0, transcendentals=0),
    )(scalars, *args)


def whole(a=None):
    return pl.BlockSpec(memory_space=pltpu.VMEM)


def turn_kernel(firsts, x_ref, *outs):
    for n, o_ref in enumerate(outs):
        for i in range(o_ref.shape[0] // 128):
            part = x_ref[:, pl.ds(pl.multiple_of(firsts[n] + i * 128, 128), 128)].astype(f32)
            tall = jnp.concatenate([part, jnp.zeros((wide - rows, 128), f32)], 0)
            o_ref[pl.ds(i * 128, 128), :] = tall.T.astype(bf16)


def turned(x, firsts, counts):
    shapes = [jax.ShapeDtypeStruct((n, wide), bf16) for n in counts]
    return call(turn_kernel, firsts, (x,), [whole()], [whole() for _ in counts], shapes, 8)


def small(kernel, sc, args, shapes, limit=6):
    shapes = [jax.ShapeDtypeStruct(*s) for s in shapes]
    return call(kernel, sc, args, [whole() for _ in args], [whole() for _ in shapes], shapes, limit)


def join_kernel(sc, *refs):
    at = 0
    for part in refs[:-1]:
        refs[-1][:, at : at + part.shape[1]] = part[...]
        at += part.shape[1]


def joined(sc, *parts):
    width = sum(p.shape[1] for p in parts)
    return small(join_kernel, sc, parts, [((parts[0].shape[0], width), bf16)])[0]


def split_kernel(sc, keep, got, here, away):
    l = sc[1]
    here[...] = keep[l] + got[l].astype(f32)
    away[...] = (keep[1 - l] + got[1 - l].astype(f32)).astype(bf16)


def add_kernel(sc, one, two, *outs):
    total = one[...] + two[...].astype(f32)
    for o_ref in outs:
        o_ref[...] = total.astype(o_ref.dtype)


def last_kernel(sc, spread, *refs):
    o_ref, at = refs[-1], 0
    for here, there in zip(refs[:-1:2], refs[1:-1:2]):
        lanes = slice(at, at + here.shape[1])
        o_ref[:, lanes] = (here[...] + there[...].astype(f32) + spread[:, lanes]).astype(bf16)
        at += here.shape[1]


def to_planes(src, dst, height):
    for s in range(tiles - 1):
        dst[pl.ds(s * height, height), :] = src[:, s * 128 : (s + 1) * 128].astype(f32)
    last = src[:, (tiles - 1) * 128 :].astype(f32)
    if last.shape[1] < 128:
        last = jnp.concatenate([last, jnp.zeros((height, 128 - last.shape[1]), f32)], 1)
    dst[pl.ds((tiles - 1) * height, height), :] = last


def every_eighth(planes, height, child, count):
    parts = [planes[pl.ds(s * height + child, count, stride=8), :] for s in range(tiles)]
    return jnp.concatenate(parts, 1).astype(bf16)


def up_kernel(sc, ops, other, *refs):
    mine, o_ref, op_planes, box_planes = refs[:-3], refs[-3], refs[-2], refs[-1]
    to_planes(ops, op_planes, 8 * share)
    for s in range(tiles):
        lanes = slice(s * 128, (s + 1) * 128)
        for i, part in enumerate(mine):
            at = pl.multiple_of(s * boxes + sc[0] * half + i * chunk, chunk)
            box_planes[pl.ds(at, chunk), :] = part[:, lanes].astype(f32)
        at = pl.multiple_of(s * boxes + (1 - sc[0]) * half, half)
        box_planes[pl.ds(at, half), :] = other[:, lanes].astype(f32)
    total = None
    for child in range(8):
        left = every_eighth(op_planes, 8 * share, child, share)
        right = every_eighth(box_planes, boxes, child, parents)
        term = lax.dot_general(left, right, (((1,), (1,)), ((), ())), preferred_element_type=f32)
        total = term if total is None else total + term
    o_ref[...] = total.astype(bf16)


def parent_rows(sc, ops, mine, other):
    args = (ops, other, *mine)
    return call(
        up_kernel,
        sc,
        args,
        [whole(a) for a in args],
        whole(),
        jax.ShapeDtypeStruct((share, parents), bf16),
        14,
        scratch=[
            pltpu.VMEM((tiles * 8 * share, 128), f32),
            pltpu.VMEM((tiles * boxes, 128), f32),
        ],
    )


def coarse_kernel(sc, lists, far, own, a, b, own_o, a_o, b_o, send, keep, picked, result):
    c, l = sc[0], sc[1]
    wanted = jnp.concatenate([lists[k : k + 1, :] for k in range(3)], 1)
    count = wanted.shape[1]
    spot = lax.broadcasted_iota(jnp.int32, (parents, count), 0)
    hot = jnp.concatenate(
        [
            (spot == wanted - base).astype(f32).astype(bf16)
            for base in (parents, sc[2], sc[3])
        ],
        0,
    )

    def pick(*parts):
        return jnp.dot(jnp.concatenate(parts, 1), hot, preferred_element_type=f32)

    lo, hi = slice(0, parents), slice(parents, 2 * parents)
    found = (
        (pick(own[:, lo], a[:, hi], b[:, lo]), pick(own[:, hi], a[:, lo], b[:, hi])),
        (pick(own_o[:, lo], a_o[:, hi], b_o[:, lo]), pick(own_o[:, hi], a_o[:, lo], b_o[:, hi])),
    )
    for j in range(4):
        x, y = j // 2, j % 2
        mine = jnp.where(l == x, found[0][0], found[0][1])
        theirs = jnp.where(l == x, found[1][0], found[1][1])
        picked[pl.ds(share * j, share), :] = jnp.where(c == y, mine, theirs)
    sources = picked[...].astype(bf16)
    total = None
    for k in range(3):
        term = jnp.dot(
            far[k], sources[:, k * parents : (k + 1) * parents], preferred_element_type=f32
        )
        total = term if total is None else total + term
    result[pl.ds(0, rows), :] = total * coarse_scale
    result[pl.ds(rows, wide - rows), :] = jnp.zeros((wide - rows, parents), f32)
    part = wide // 2
    keep[...] = result[pl.ds(pl.multiple_of(c * part, part), part), :]
    send[...] = result[pl.ds(pl.multiple_of((1 - c) * part, part), part), :].astype(bf16)


def coarse_partial(sc, lists, far, own, a, b, own_o, a_o, b_o):
    args = (lists, far, own, a, b, own_o, a_o, b_o)
    shape = (wide // 2, parents)
    return call(
        coarse_kernel,
        sc,
        args,
        [whole(x) for x in args],
        [whole(), whole()],
        [jax.ShapeDtypeStruct(shape, bf16), jax.ShapeDtypeStruct(shape, f32)],
        8,
        scratch=[pltpu.VMEM((rows, 3 * parents), f32), pltpu.VMEM((wide, parents), f32)],
    )


def down_kernel(sc, ops, mine, other, o_ref, op_planes, check, turned_rows):
    c, part = sc[0], wide // 2
    to_planes(ops, op_planes, 8 * share)
    check[pl.ds(pl.multiple_of(c * part, part), part), :] = mine[...]
    check[pl.ds(pl.multiple_of((1 - c) * part, part), part), :] = other[...]
    whole_check = check[...]
    for child in range(8):
        left = every_eighth(op_planes, 8 * share, child, share)
        z = jnp.dot(left, whole_check, preferred_element_type=f32)
        z = jnp.concatenate([z, jnp.zeros((256 - share, parents), f32)], 0).T
        for t in (0, 1):
            turned_rows[pl.ds(t * boxes + child, parents, stride=8), :] = z[
                :, t * 128 : (t + 1) * 128
            ]
    o_ref[pl.ds(0, 128), :] = turned_rows[pl.ds(0, boxes), :].T
    o_ref[pl.ds(128, share - 128), :] = turned_rows[pl.ds(boxes, boxes), :].T[: share - 128]


def downward(sc, ops, mine, other):
    args = (ops, mine, other)
    return call(
        down_kernel,
        sc,
        args,
        [whole(x) for x in args],
        whole(),
        jax.ShapeDtypeStruct((share, boxes), f32),
        12,
        scratch=[
            pltpu.VMEM((tiles * 8 * share, 128), f32),
            pltpu.VMEM((wide, parents), bf16),
            pltpu.VMEM((2 * boxes, 128), f32),
        ],
    )


pitch, step_boxes, unroll = early + 8, 512, 32


def gather_kernel(spots, *refs):
    pieces, o_ref, planes, got = refs[:-3], refs[-3], refs[-2], refs[-1]
    step = pl.program_id(0)
    depth = step_boxes + 8

    @pl.when(step == 0)
    def _():
        at = 0
        for piece in pieces:
            count = piece.shape[0]
            for s in range(tiles):
                planes[pl.ds(s * pitch + at, count), :] = piece[
                    :, s * 128 : (s + 1) * 128
                ].astype(f32)
            at += count
        for s in range(tiles):
            planes[pl.ds(s * pitch + early, 8), :] = jnp.zeros((8, 128), f32)

    def body(i, carry):
        found = [
            planes[pl.ds(spots[step * step_boxes + i * unroll + u], 8, stride=pitch), :]
            for u in range(unroll)
        ]
        for u in range(unroll):
            got[pl.ds(i * unroll + u, 8, stride=depth), :] = found[u]
        return carry

    lax.fori_loop(0, step_boxes // unroll, body, 0)
    for s in range(tiles):
        spot = pl.ds(pl.multiple_of(step * step_boxes, step_boxes), step_boxes)
        o_ref[spot, s * 128 : (s + 1) * 128] = got[pl.ds(s * depth, step_boxes), :].astype(bf16)


def gathered(spots, pieces):
    return call(
        gather_kernel,
        spots,
        tuple(pieces),
        [whole(p) for p in pieces],
        whole(),
        jax.ShapeDtypeStruct((3 * boxes, wide), bf16),
        16,
        grid=(3 * boxes // step_boxes,),
        scratch=[
            pltpu.VMEM((8 * pitch, 128), f32),
            pltpu.VMEM((8 * (step_boxes + 8), 128), f32),
        ],
    )


def far_kernel(start, sc, far, sources, lists, late, late_o, send, keep, result):
    c = sc[0]
    count, most = send.shape[2], result.shape[1]
    late_boxes = jnp.concatenate([late[...], late_o[...]], 0)

    def tile(at, width):
        spot = lax.broadcasted_iota(jnp.int32, (width, 128), 1).astype(f32)
        total = None
        for k in range(3):
            listed = lists[k : k + 1, start + at : start + at + width].astype(f32)
            wanted = jnp.broadcast_to(listed, (128, width)).T
            hot = jnp.concatenate(
                [
                    (wanted == spot + float(base)).astype(f32).astype(bf16)
                    for base in range(0, 2 * chunk, 128)
                ],
                1,
            )
            found = jnp.dot(hot, late_boxes, preferred_element_type=f32)
            found = found + sources[pl.ds(k * boxes + start + at, width), :].astype(f32)
            term = lax.dot_general(
                far[k],
                found.astype(bf16)[:, :rows],
                (((1,), (1,)), ((), ())),
                preferred_element_type=f32,
            )
            total = term if total is None else total + term
        result[:, :width] = total
        lanes = slice(at, at + width)
        for x in (0, 1):
            first = result[pl.ds(share * 2 * x, share), :width]
            second = result[pl.ds(share * (2 * x + 1), share), :width]
            keep[x, :, lanes] = jnp.where(c == 0, first, second)
            send[x, :, lanes] = jnp.where(c == 0, second, first).astype(bf16)

    for at in range(0, count, most):
        tile(at, min(most, count - at))


def far_partial(sc, far, sources, lists, late, late_o, start, count):
    shape = (2, share, count)
    args = (far, sources, lists, late, late_o)
    return call(
        functools.partial(far_kernel, start),
        sc,
        args,
        [whole(x) for x in args],
        [whole(), whole()],
        [jax.ShapeDtypeStruct(shape, bf16), jax.ShapeDtypeStruct(shape, f32)],
        12,
        scratch=[pltpu.VMEM((rows, 256), f32)],
    )


def after(x, *others):
    return lax.optimization_barrier((x, *others))[0]


def local(leaf_density, upward_ops, far_ops, downward_ops, fine_lists, coarse_lists):
    groups = lax.axis_size("space")
    group, rep = lax.axis_index("space"), lax.axis_index("rep")
    l, c = rep >> 1, rep & 1
    no_previous, no_next = group == 0, group == groups - 1
    nowhere = -16384
    base_previous = jnp.where(no_previous, nowhere, 0)
    base_next = jnp.where(no_next, nowhere, 2 * parents)
    sc = jnp.stack(
        [
            c,
            l,
            jnp.where(l == 0, base_previous, base_next),
            jnp.where(l == 0, base_next, base_previous),
        ]
    ).astype(jnp.int32)
    hop = functools.partial(lax.ppermute, axis_name=both, perm=one_hop(groups))
    zswap = functools.partial(lax.ppermute, axis_name=both, perm=across(groups, 2))
    cswap = functools.partial(lax.ppermute, axis_name=both, perm=across(groups, 1))

    def at(i):
        return jnp.reshape(i, (1,)).astype(jnp.int32)

    up_ops = jnp.transpose(upward_ops, (1, 0, 2)).reshape(8 * share, rows)
    down_ops = jnp.transpose(downward_ops, (1, 0, 2)).reshape(8 * share, rows)

    which, side, offset = fine_lists >> 10, (fine_lists >> 9) & 1, fine_lists & (half - 1)
    outside = ((which == 0) & no_previous) | ((which == 2) & no_next)
    direct = (which == 0) == (l == 0)
    theirs = (side != c).astype(jnp.int32)
    is_late = (which != 1) & ~direct & (offset >= half - chunk)
    spots = jnp.where(
        which == 1,
        theirs * half + offset,
        jnp.where(
            direct,
            2 * half + theirs * half + offset,
            4 * half + theirs * (half - chunk) + offset,
        ),
    )
    spots = jnp.where(outside | is_late, early, spots).reshape(-1)
    late_lists = jnp.where(is_late & ~outside, theirs * chunk + offset - (half - chunk), -1)

    head = turned(leaf_density, at(c * half), [chunk])[0]
    rest = [c * half + i * chunk for i in range(1, chunks)] + [(1 - c) * half]
    rest = jnp.stack(rest).astype(jnp.int32)
    *tails, other = turned(leaf_density, after(rest, head), [chunk] * (chunks - 1) + [half])
    up = parent_rows(after(sc, spots, late_lists), up_ops, [head, *tails], other)
    own = joined(sc, up, zswap(up))
    ca = hop(own)
    own_o = cswap(own)
    mine = [head, tails[0], after(tails[1], up), after(tails[2], own)]
    a = [hop(m) for m in mine]
    came, b = [], []
    for i, x in enumerate(a):
        earlier = (up, own, own_o)[: i + 1] + tuple(came[-1:]) + tuple(b[i - 2 : i - 1] if i > 1 else ())
        came.append(after(x, *earlier))
        b.append(zswap(came[-1]))
    came[-1] = after(came[-1], ca, b[-2])
    a_o = [cswap(x) for x in came]
    cb, ca_o = zswap(ca), cswap(ca)
    b_o = [cswap(x) for x in b[:-1]]
    picked = gathered(spots, [*mine, other, *a, *a_o, *b[:-1], *b_o])
    b_o.append(cswap(after(b[-1], picked, cb)))
    cb_o = cswap(cb)

    def summed(send, keep):
        shape = (share, send.shape[2])
        here, away = small(split_kernel, sc, (keep, cswap(send)), [(shape, f32), (shape, bf16)])
        return here, zswap(away), away

    late = (b[-1], b_o[-1])
    send, keep = far_partial(sc, far_ops, picked, late_lists, *late, 0, ahead)
    left = summed(after(send, cb_o, ca_o), keep)
    send, keep = coarse_partial(
        after(sc, send), coarse_lists, far_ops, own, ca, cb, own_o, ca_o, cb_o
    )
    shape = (wide // 2, parents)
    part, part_sent = small(
        add_kernel, after(sc, left[2]), (keep, cswap(send)), [(shape, f32), (shape, bf16)]
    )
    send, keep = far_partial(
        after(sc, part), far_ops, picked, late_lists, *late, ahead, boxes - ahead
    )
    part_got = zswap(part_sent)
    right = summed(after(send, left[1], part_got), keep)
    check = small(add_kernel, sc, (part, part_got), [(shape, bf16)])[0]
    check_o = cswap(check)
    spread = downward(after(sc, right[2]), down_ops, check, check_o)
    return small(last_kernel, sc, (spread, *left[:2], *right[:2]), [((share, boxes), bf16)])[0]


def solution(mesh):
    return jax.shard_map(
        local,
        mesh=mesh,
        in_specs=(
            P(None, "space"),
            P(None, "rep", None),
            P("rep", None, None),
            P(None, "rep", None),
            P("rep", "space"),
            P("rep", "space"),
        ),
        out_specs=P("rep", "space"),
        check_vma=False,
    )
```

```python
import functools

import jax
import jax.numpy as jnp
from jax import lax
from jax.experimental import pallas as pl
from jax.experimental.pallas import tpu as pltpu
from jax.sharding import PartitionSpec as P

bf16, f32 = jnp.bfloat16, jnp.float32
both = ("space", "rep")
coarse_scale = 0.5
rows, wide, tiles = 888, 896, 7
boxes, half = 1024, 512
parents = 128
share, share_pad = 222, 224
coarse_block = wide // 8
chunks = 2
chunk = half // chunks
early = 6 * half - 2 * chunk
ahead = 512


def one_hop(groups):
    up = [(4 * s + 2 + c, 4 * (s + 1) + c) for s in range(groups - 1) for c in (0, 1)]
    up += [(0, 1), (4 * groups - 2, 4 * groups - 1)]
    return up + [(j, i) for i, j in up]


def across(groups, flip):
    return [(4 * s + r, 4 * s + (r ^ flip)) for s in range(groups) for r in range(4)]


def call(kernel, scalars, args, in_specs, out_specs, out_shape, limit, grid=(1,), scratch=()):
    return pl.pallas_call(
        kernel,
        grid_spec=pltpu.PrefetchScalarGridSpec(
            num_scalar_prefetch=1,
            grid=grid,
            in_specs=in_specs,
            out_specs=out_specs,
            scratch_shapes=scratch,
        ),
        out_shape=out_shape,
        compiler_params=pltpu.CompilerParams(vmem_limit_bytes=limit << 20),
        cost_estimate=pl.CostEstimate(flops=0, bytes_accessed=0, transcendentals=0),
    )(scalars, *args)


def whole(a=None):
    return pl.BlockSpec(memory_space=pltpu.VMEM)


def turn_kernel(firsts, x_ref, *outs):
    for n, o_ref in enumerate(outs):
        for i in range(o_ref.shape[0] // 128):
            part = x_ref[:, pl.ds(pl.multiple_of(firsts[n] + i * 128, 128), 128)].astype(f32)
            tall = jnp.concatenate([part, jnp.zeros((wide - rows, 128), f32)], 0)
            o_ref[pl.ds(i * 128, 128), :] = tall.T.astype(bf16)


def turned(x, firsts, counts):
    shapes = [jax.ShapeDtypeStruct((n, wide), bf16) for n in counts]
    return call(turn_kernel, firsts, (x,), [whole()], [whole() for _ in counts], shapes, 8)


def small(kernel, sc, args, shapes, limit=6):
    shapes = [jax.ShapeDtypeStruct(*s) for s in shapes]
    return call(kernel, sc, args, [whole() for _ in args], [whole() for _ in shapes], shapes, limit)


def join_kernel(sc, *refs):
    at = 0
    for part in refs[:-1]:
        refs[-1][:, at : at + part.shape[1]] = part[...]
        at += part.shape[1]


def joined(sc, *parts):
    width = sum(p.shape[1] for p in parts)
    return small(join_kernel, sc, parts, [((parts[0].shape[0], width), bf16)])[0]


def split_kernel(sc, keep, got, here, away):
    l = sc[1]
    here[...] = keep[l] + got[l].astype(f32)
    away[...] = (keep[1 - l] + got[1 - l].astype(f32)).astype(bf16)


def split_both_kernel(sc, keep, got, coarse_keep, coarse_got, here, away, part):
    l = sc[1]
    here[...] = keep[l] + got[l].astype(f32)
    theirs = keep[1 - l] + got[1 - l].astype(f32)
    theirs = jnp.concatenate([theirs, jnp.zeros((share_pad - share, theirs.shape[1]), f32)], 0)
    away[:share_pad, :] = theirs.astype(bf16)
    total = coarse_keep[...] + coarse_got[...].astype(f32)
    part[...] = total
    for i in range(4):
        block = total[i * coarse_block : (i + 1) * coarse_block]
        away[share_pad:, i * parents : (i + 1) * parents] = block.astype(bf16)


def check_kernel(sc, part, got, o_ref):
    for i in range(4):
        lines = slice(i * coarse_block, (i + 1) * coarse_block)
        theirs = got[share_pad:, i * parents : (i + 1) * parents].astype(f32)
        o_ref[lines, :] = (part[lines, :] + theirs).astype(bf16)


def last_kernel(sc, spread, *refs):
    o_ref, at = refs[-1], 0
    for here, there in zip(refs[:-1:2], refs[1:-1:2]):
        lanes = slice(at, at + here.shape[1])
        o_ref[:, lanes] = (here[...] + there[:share, :].astype(f32) + spread[:, lanes]).astype(bf16)
        at += here.shape[1]


def to_planes(src, dst, height):
    for s in range(tiles - 1):
        dst[pl.ds(s * height, height), :] = src[:, s * 128 : (s + 1) * 128].astype(f32)
    last = src[:, (tiles - 1) * 128 :].astype(f32)
    if last.shape[1] < 128:
        last = jnp.concatenate([last, jnp.zeros((height, 128 - last.shape[1]), f32)], 1)
    dst[pl.ds((tiles - 1) * height, height), :] = last


def every_eighth(planes, height, child, count):
    parts = [planes[pl.ds(s * height + child, count, stride=8), :] for s in range(tiles)]
    return jnp.concatenate(parts, 1).astype(bf16)


def up_kernel(sc, ops, other, *refs):
    mine, o_ref, op_planes, box_planes = refs[:-3], refs[-3], refs[-2], refs[-1]
    to_planes(ops, op_planes, 8 * share)
    for s in range(tiles):
        lanes = slice(s * 128, (s + 1) * 128)
        for i, part in enumerate(mine):
            at = pl.multiple_of(s * boxes + sc[0] * half + i * chunk, chunk)
            box_planes[pl.ds(at, chunk), :] = part[:, lanes].astype(f32)
        at = pl.multiple_of(s * boxes + (1 - sc[0]) * half, half)
        box_planes[pl.ds(at, half), :] = other[:, lanes].astype(f32)
    total = None
    for child in range(8):
        left = every_eighth(op_planes, 8 * share, child, share)
        right = every_eighth(box_planes, boxes, child, parents)
        term = lax.dot_general(left, right, (((1,), (1,)), ((), ())), preferred_element_type=f32)
        total = term if total is None else total + term
    o_ref[...] = total.astype(bf16)


def parent_rows(sc, ops, mine, other):
    args = (ops, other, *mine)
    return call(
        up_kernel,
        sc,
        args,
        [whole(a) for a in args],
        whole(),
        jax.ShapeDtypeStruct((share, parents), bf16),
        14,
        scratch=[
            pltpu.VMEM((tiles * 8 * share, 128), f32),
            pltpu.VMEM((tiles * boxes, 128), f32),
        ],
    )


def coarse_kernel(sc, lists, far, own, a, b, own_o, a_o, b_o, send, keep, picked, result):
    c, l = sc[0], sc[1]
    wanted = jnp.concatenate([lists[k : k + 1, :] for k in range(3)], 1)
    count = wanted.shape[1]
    spot = lax.broadcasted_iota(jnp.int32, (parents, count), 0)
    hot = jnp.concatenate(
        [
            (spot == wanted - base).astype(f32).astype(bf16)
            for base in (parents, sc[2], sc[3])
        ],
        0,
    )

    def pick(*parts):
        return jnp.dot(jnp.concatenate(parts, 1), hot, preferred_element_type=f32)

    lo, hi = slice(0, parents), slice(parents, 2 * parents)
    found = (
        (pick(own[:, lo], a[:, hi], b[:, lo]), pick(own[:, hi], a[:, lo], b[:, hi])),
        (pick(own_o[:, lo], a_o[:, hi], b_o[:, lo]), pick(own_o[:, hi], a_o[:, lo], b_o[:, hi])),
    )
    for j in range(4):
        x, y = j // 2, j % 2
        mine = jnp.where(l == x, found[0][0], found[0][1])
        theirs = jnp.where(l == x, found[1][0], found[1][1])
        picked[pl.ds(share * j, share), :] = jnp.where(c == y, mine, theirs)
    sources = picked[...].astype(bf16)
    total = None
    for k in range(3):
        term = jnp.dot(
            far[k], sources[:, k * parents : (k + 1) * parents], preferred_element_type=f32
        )
        total = term if total is None else total + term
    result[pl.ds(0, rows), :] = total * coarse_scale
    result[pl.ds(rows, wide - rows), :] = jnp.zeros((wide - rows, parents), f32)
    part = wide // 2
    keep[...] = result[pl.ds(pl.multiple_of(c * part, part), part), :]
    send[...] = result[pl.ds(pl.multiple_of((1 - c) * part, part), part), :].astype(bf16)


def coarse_partial(sc, lists, far, own, a, b, own_o, a_o, b_o):
    args = (lists, far, own, a, b, own_o, a_o, b_o)
    shape = (wide // 2, parents)
    return call(
        coarse_kernel,
        sc,
        args,
        [whole(x) for x in args],
        [whole(), whole()],
        [jax.ShapeDtypeStruct(shape, bf16), jax.ShapeDtypeStruct(shape, f32)],
        8,
        scratch=[pltpu.VMEM((rows, 3 * parents), f32), pltpu.VMEM((wide, parents), f32)],
    )


def down_kernel(sc, ops, mine, other, o_ref, op_planes, check, turned_rows):
    c, part = sc[0], wide // 2
    to_planes(ops, op_planes, 8 * share)
    check[pl.ds(pl.multiple_of(c * part, part), part), :] = mine[...]
    check[pl.ds(pl.multiple_of((1 - c) * part, part), part), :] = other[...]
    whole_check = check[...]
    for child in range(8):
        left = every_eighth(op_planes, 8 * share, child, share)
        z = jnp.dot(left, whole_check, preferred_element_type=f32)
        z = jnp.concatenate([z, jnp.zeros((256 - share, parents), f32)], 0).T
        for t in (0, 1):
            turned_rows[pl.ds(t * boxes + child, parents, stride=8), :] = z[
                :, t * 128 : (t + 1) * 128
            ]
    o_ref[pl.ds(0, 128), :] = turned_rows[pl.ds(0, boxes), :].T
    o_ref[pl.ds(128, share - 128), :] = turned_rows[pl.ds(boxes, boxes), :].T[: share - 128]


def downward(sc, ops, mine, other):
    args = (ops, mine, other)
    return call(
        down_kernel,
        sc,
        args,
        [whole(x) for x in args],
        whole(),
        jax.ShapeDtypeStruct((share, boxes), f32),
        12,
        scratch=[
            pltpu.VMEM((tiles * 8 * share, 128), f32),
            pltpu.VMEM((wide, parents), bf16),
            pltpu.VMEM((2 * boxes, 128), f32),
        ],
    )


pitch, step_boxes, unroll = early + 8, 512, 32


def gather_kernel(spots, *refs):
    pieces, o_ref, planes, got = refs[:-3], refs[-3], refs[-2], refs[-1]
    step = pl.program_id(0)
    depth = step_boxes + 8

    @pl.when(step == 0)
    def _():
        at = 0
        for piece in pieces:
            count = piece.shape[0]
            for s in range(tiles):
                planes[pl.ds(s * pitch + at, count), :] = piece[
                    :, s * 128 : (s + 1) * 128
                ].astype(f32)
            at += count
        for s in range(tiles):
            planes[pl.ds(s * pitch + early, 8), :] = jnp.zeros((8, 128), f32)

    def body(i, carry):
        found = [
            planes[pl.ds(spots[step * step_boxes + i * unroll + u], 8, stride=pitch), :]
            for u in range(unroll)
        ]
        for u in range(unroll):
            got[pl.ds(i * unroll + u, 8, stride=depth), :] = found[u]
        return carry

    lax.fori_loop(0, step_boxes // unroll, body, 0)
    for s in range(tiles):
        spot = pl.ds(pl.multiple_of(step * step_boxes, step_boxes), step_boxes)
        o_ref[spot, s * 128 : (s + 1) * 128] = got[pl.ds(s * depth, step_boxes), :].astype(bf16)


def gathered(spots, pieces):
    return call(
        gather_kernel,
        spots,
        tuple(pieces),
        [whole(p) for p in pieces],
        whole(),
        jax.ShapeDtypeStruct((3 * boxes, wide), bf16),
        16,
        grid=(3 * boxes // step_boxes,),
        scratch=[
            pltpu.VMEM((8 * pitch, 128), f32),
            pltpu.VMEM((8 * (step_boxes + 8), 128), f32),
        ],
    )


def far_kernel(start, sc, far, sources, lists, late, late_o, send, keep, result):
    c = sc[0]
    count, most = send.shape[2], result.shape[1]
    late_boxes = jnp.concatenate([late[...], late_o[...]], 0)

    def tile(at, width):
        spot = lax.broadcasted_iota(jnp.int32, (width, 128), 1).astype(f32)
        total = None
        for k in range(3):
            listed = lists[k : k + 1, start + at : start + at + width].astype(f32)
            wanted = jnp.broadcast_to(listed, (128, width)).T
            hot = jnp.concatenate(
                [
                    (wanted == spot + float(base)).astype(f32).astype(bf16)
                    for base in range(0, 2 * chunk, 128)
                ],
                1,
            )
            found = jnp.dot(hot, late_boxes, preferred_element_type=f32)
            found = found + sources[pl.ds(k * boxes + start + at, width), :].astype(f32)
            term = lax.dot_general(
                far[k],
                found.astype(bf16)[:, :rows],
                (((1,), (1,)), ((), ())),
                preferred_element_type=f32,
            )
            total = term if total is None else total + term
        result[:, :width] = total
        lanes = slice(at, at + width)
        for x in (0, 1):
            first = result[pl.ds(share * 2 * x, share), :width]
            second = result[pl.ds(share * (2 * x + 1), share), :width]
            keep[x, :, lanes] = jnp.where(c == 0, first, second)
            send[x, :, lanes] = jnp.where(c == 0, second, first).astype(bf16)

    for at in range(0, count, most):
        tile(at, min(most, count - at))


def far_partial(sc, far, sources, lists, late, late_o, start, count):
    shape = (2, share, count)
    args = (far, sources, lists, late, late_o)
    return call(
        functools.partial(far_kernel, start),
        sc,
        args,
        [whole(x) for x in args],
        [whole(), whole()],
        [jax.ShapeDtypeStruct(shape, bf16), jax.ShapeDtypeStruct(shape, f32)],
        12,
        scratch=[pltpu.VMEM((rows, 256), f32)],
    )


def after(x, *others):
    return lax.optimization_barrier((x, *others))[0]


def local(leaf_density, upward_ops, far_ops, downward_ops, fine_lists, coarse_lists):
    groups = lax.axis_size("space")
    group, rep = lax.axis_index("space"), lax.axis_index("rep")
    l, c = rep >> 1, rep & 1
    no_previous, no_next = group == 0, group == groups - 1
    nowhere = -16384
    base_previous = jnp.where(no_previous, nowhere, 0)
    base_next = jnp.where(no_next, nowhere, 2 * parents)
    sc = jnp.stack(
        [
            c,
            l,
            jnp.where(l == 0, base_previous, base_next),
            jnp.where(l == 0, base_next, base_previous),
        ]
    ).astype(jnp.int32)
    hop = functools.partial(lax.ppermute, axis_name=both, perm=one_hop(groups))
    zswap = functools.partial(lax.ppermute, axis_name=both, perm=across(groups, 2))
    cswap = functools.partial(lax.ppermute, axis_name=both, perm=across(groups, 1))

    def at(i):
        return jnp.reshape(i, (1,)).astype(jnp.int32)

    up_ops = jnp.transpose(upward_ops, (1, 0, 2)).reshape(8 * share, rows)
    down_ops = jnp.transpose(downward_ops, (1, 0, 2)).reshape(8 * share, rows)

    which, side, offset = fine_lists >> 10, (fine_lists >> 9) & 1, fine_lists & (half - 1)
    outside = ((which == 0) & no_previous) | ((which == 2) & no_next)
    direct = (which == 0) == (l == 0)
    theirs = (side != c).astype(jnp.int32)
    is_late = (which != 1) & ~direct & (offset >= half - chunk)
    spots = jnp.where(
        which == 1,
        theirs * half + offset,
        jnp.where(
            direct,
            2 * half + theirs * half + offset,
            4 * half + theirs * (half - chunk) + offset,
        ),
    )
    spots = jnp.where(outside | is_late, early, spots).reshape(-1)
    late_lists = jnp.where(is_late & ~outside, theirs * chunk + offset - (half - chunk), -1)

    head = turned(leaf_density, at(c * half), [chunk])[0]
    rest = jnp.stack([c * half + chunk, (1 - c) * half]).astype(jnp.int32)
    tail, other = turned(leaf_density, after(rest, head), [half - chunk, half])
    up = parent_rows(after(sc, spots, late_lists), up_ops, [head, tail], other)
    own = joined(sc, up, zswap(up))
    ca = hop(own)
    own_o = cswap(own)
    mine = [head, after(tail, up)]
    a = [hop(m) for m in mine]
    early_a = after(a[0], own)
    second = after(a[1], early_a, own_o)
    b = [zswap(early_a), zswap(second)]
    a_o = [cswap(early_a), cswap(after(second, ca))]
    cb, ca_o = zswap(ca), cswap(ca)
    b_o = [cswap(b[0])]
    picked = gathered(spots, [*mine, other, *a, *a_o, b[0], b_o[0]])
    b_o.append(cswap(after(b[1], picked)))
    cb_o = cswap(cb)

    late = (b[1], b_o[1])
    send, keep = far_partial(sc, far_ops, picked, late_lists, *late, 0, ahead)
    got = cswap(after(send, cb, ca_o))
    coarse_send, coarse_keep = coarse_partial(
        after(sc, send), coarse_lists, far_ops, own, ca, cb, own_o, ca_o, cb_o
    )
    here, away, part = small(
        split_both_kernel,
        sc,
        (keep, got, coarse_keep, cswap(coarse_send)),
        [
            ((share, ahead), f32),
            ((share_pad + coarse_block, ahead), bf16),
            ((wide // 2, parents), f32),
        ],
    )
    left = here, zswap(away)
    send, keep = far_partial(
        after(sc, part), far_ops, picked, late_lists, *late, ahead, boxes - ahead
    )
    shape = (share, boxes - ahead)
    here, away = small(
        split_kernel, sc, (keep, cswap(after(send, left[1]))), [(shape, f32), (shape, bf16)]
    )
    right = here, zswap(away)
    check = small(check_kernel, sc, (part, left[1]), [((wide // 2, parents), bf16)])[0]
    check_o = cswap(check)
    spread = downward(after(sc, away), down_ops, check, check_o)
    return small(last_kernel, sc, (spread, *left, *right), [((share, boxes), bf16)])[0]


def solution(mesh):
    return jax.shard_map(
        local,
        mesh=mesh,
        in_specs=(
            P(None, "space"),
            P(None, "rep", None),
            P("rep", None, None),
            P(None, "rep", None),
            P("rep", "space"),
            P("rep", "space"),
        ),
        out_specs=P("rep", "space"),
        check_vma=False,
    )
```

```python
import functools

import jax
import jax.numpy as jnp
from jax import lax
from jax.experimental import pallas as pl
from jax.experimental.pallas import tpu as pltpu
from jax.sharding import PartitionSpec as P

bf16, f32 = jnp.bfloat16, jnp.float32
both = ("space", "rep")
coarse_scale = 0.5
rows, wide, tiles = 888, 896, 7
boxes, half = 1024, 512
parents = 128
share = 222
chunks = 2
chunk = half // chunks
early = 6 * half - 2 * chunk
ahead = 512


def one_hop(groups):
    up = [(4 * s + 2 + c, 4 * (s + 1) + c) for s in range(groups - 1) for c in (0, 1)]
    up += [(0, 1), (4 * groups - 2, 4 * groups - 1)]
    return up + [(j, i) for i, j in up]


def across(groups, flip):
    return [(4 * s + r, 4 * s + (r ^ flip)) for s in range(groups) for r in range(4)]


def call(kernel, scalars, args, in_specs, out_specs, out_shape, limit, grid=(1,), scratch=()):
    return pl.pallas_call(
        kernel,
        grid_spec=pltpu.PrefetchScalarGridSpec(
            num_scalar_prefetch=1,
            grid=grid,
            in_specs=in_specs,
            out_specs=out_specs,
            scratch_shapes=scratch,
        ),
        out_shape=out_shape,
        compiler_params=pltpu.CompilerParams(vmem_limit_bytes=limit << 20),
        cost_estimate=pl.CostEstimate(flops=0, bytes_accessed=0, transcendentals=0),
    )(scalars, *args)


def whole(a=None):
    return pl.BlockSpec(memory_space=pltpu.VMEM)


def turn_kernel(firsts, x_ref, *outs):
    for n, o_ref in enumerate(outs):
        for i in range(o_ref.shape[0] // 128):
            part = x_ref[:, pl.ds(pl.multiple_of(firsts[n] + i * 128, 128), 128)].astype(f32)
            tall = jnp.concatenate([part, jnp.zeros((wide - rows, 128), f32)], 0)
            o_ref[pl.ds(i * 128, 128), :] = tall.T.astype(bf16)


def turned(x, firsts, counts):
    shapes = [jax.ShapeDtypeStruct((n, wide), bf16) for n in counts]
    return call(turn_kernel, firsts, (x,), [whole()], [whole() for _ in counts], shapes, 8)


def small(kernel, sc, args, shapes, limit=6):
    shapes = [jax.ShapeDtypeStruct(*s) for s in shapes]
    return call(kernel, sc, args, [whole() for _ in args], [whole() for _ in shapes], shapes, limit)


def join_kernel(sc, *refs):
    at = 0
    for part in refs[:-1]:
        refs[-1][:, at : at + part.shape[1]] = part[...]
        at += part.shape[1]


def joined(sc, *parts):
    width = sum(p.shape[1] for p in parts)
    return small(join_kernel, sc, parts, [((parts[0].shape[0], width), bf16)])[0]


def split_kernel(sc, keep, got, here, away):
    l = sc[1]
    here[...] = keep[l] + got[l].astype(f32)
    away[...] = (keep[1 - l] + got[1 - l].astype(f32)).astype(bf16)


def add_kernel(sc, one, two, *outs):
    total = one[...] + two[...].astype(f32)
    for o_ref in outs:
        o_ref[...] = total.astype(o_ref.dtype)


def last_kernel(sc, spread, *refs):
    o_ref, at = refs[-1], 0
    for here, there in zip(refs[:-1:2], refs[1:-1:2]):
        lanes = slice(at, at + here.shape[1])
        o_ref[:, lanes] = (here[...] + there[...].astype(f32) + spread[:, lanes]).astype(bf16)
        at += here.shape[1]


def to_planes(src, dst, height):
    for s in range(tiles - 1):
        dst[pl.ds(s * height, height), :] = src[:, s * 128 : (s + 1) * 128].astype(f32)
    last = src[:, (tiles - 1) * 128 :].astype(f32)
    if last.shape[1] < 128:
        last = jnp.concatenate([last, jnp.zeros((height, 128 - last.shape[1]), f32)], 1)
    dst[pl.ds((tiles - 1) * height, height), :] = last


def every_eighth(planes, height, child, count):
    parts = [planes[pl.ds(s * height + child, count, stride=8), :] for s in range(tiles)]
    return jnp.concatenate(parts, 1).astype(bf16)


def up_kernel(sc, ops, other, *refs):
    mine, o_ref, op_planes, box_planes = refs[:-3], refs[-3], refs[-2], refs[-1]
    to_planes(ops, op_planes, 8 * share)
    for s in range(tiles):
        lanes = slice(s * 128, (s + 1) * 128)
        for i, part in enumerate(mine):
            at = pl.multiple_of(s * boxes + sc[0] * half + i * chunk, chunk)
            box_planes[pl.ds(at, chunk), :] = part[:, lanes].astype(f32)
        at = pl.multiple_of(s * boxes + (1 - sc[0]) * half, half)
        box_planes[pl.ds(at, half), :] = other[:, lanes].astype(f32)
    total = None
    for child in range(8):
        left = every_eighth(op_planes, 8 * share, child, share)
        right = every_eighth(box_planes, boxes, child, parents)
        term = lax.dot_general(left, right, (((1,), (1,)), ((), ())), preferred_element_type=f32)
        total = term if total is None else total + term
    o_ref[...] = total.astype(bf16)


def parent_rows(sc, ops, mine, other):
    args = (ops, other, *mine)
    return call(
        up_kernel,
        sc,
        args,
        [whole(a) for a in args],
        whole(),
        jax.ShapeDtypeStruct((share, parents), bf16),
        14,
        scratch=[
            pltpu.VMEM((tiles * 8 * share, 128), f32),
            pltpu.VMEM((tiles * boxes, 128), f32),
        ],
    )


def coarse_kernel(sc, lists, far, own, a, b, own_o, a_o, b_o, send, keep, picked, result):
    c, l = sc[0], sc[1]
    wanted = jnp.concatenate([lists[k : k + 1, :] for k in range(3)], 1)
    count = wanted.shape[1]
    spot = lax.broadcasted_iota(jnp.int32, (parents, count), 0)
    hot = jnp.concatenate(
        [
            (spot == wanted - base).astype(f32).astype(bf16)
            for base in (parents, sc[2], sc[3])
        ],
        0,
    )

    def pick(*parts):
        return jnp.dot(jnp.concatenate(parts, 1), hot, preferred_element_type=f32)

    lo, hi = slice(0, parents), slice(parents, 2 * parents)
    found = (
        (pick(own[:, lo], a[:, hi], b[:, lo]), pick(own[:, hi], a[:, lo], b[:, hi])),
        (pick(own_o[:, lo], a_o[:, hi], b_o[:, lo]), pick(own_o[:, hi], a_o[:, lo], b_o[:, hi])),
    )
    for j in range(4):
        x, y = j // 2, j % 2
        mine = jnp.where(l == x, found[0][0], found[0][1])
        theirs = jnp.where(l == x, found[1][0], found[1][1])
        picked[pl.ds(share * j, share), :] = jnp.where(c == y, mine, theirs)
    sources = picked[...].astype(bf16)
    total = None
    for k in range(3):
        term = jnp.dot(
            far[k], sources[:, k * parents : (k + 1) * parents], preferred_element_type=f32
        )
        total = term if total is None else total + term
    result[pl.ds(0, rows), :] = total * coarse_scale
    result[pl.ds(rows, wide - rows), :] = jnp.zeros((wide - rows, parents), f32)
    part = wide // 2
    keep[...] = result[pl.ds(pl.multiple_of(c * part, part), part), :]
    send[...] = result[pl.ds(pl.multiple_of((1 - c) * part, part), part), :].astype(bf16)


def coarse_partial(sc, lists, far, own, a, b, own_o, a_o, b_o):
    args = (lists, far, own, a, b, own_o, a_o, b_o)
    shape = (wide // 2, parents)
    return call(
        coarse_kernel,
        sc,
        args,
        [whole(x) for x in args],
        [whole(), whole()],
        [jax.ShapeDtypeStruct(shape, bf16), jax.ShapeDtypeStruct(shape, f32)],
        8,
        scratch=[pltpu.VMEM((rows, 3 * parents), f32), pltpu.VMEM((wide, parents), f32)],
    )


def down_kernel(sc, ops, mine, other, o_ref, op_planes, check, turned_rows):
    c, part = sc[0], wide // 2
    to_planes(ops, op_planes, 8 * share)
    check[pl.ds(pl.multiple_of(c * part, part), part), :] = mine[...]
    check[pl.ds(pl.multiple_of((1 - c) * part, part), part), :] = other[...]
    whole_check = check[...]
    for child in range(8):
        left = every_eighth(op_planes, 8 * share, child, share)
        z = jnp.dot(left, whole_check, preferred_element_type=f32)
        z = jnp.concatenate([z, jnp.zeros((256 - share, parents), f32)], 0).T
        for t in (0, 1):
            turned_rows[pl.ds(t * boxes + child, parents, stride=8), :] = z[
                :, t * 128 : (t + 1) * 128
            ]
    o_ref[pl.ds(0, 128), :] = turned_rows[pl.ds(0, boxes), :].T
    o_ref[pl.ds(128, share - 128), :] = turned_rows[pl.ds(boxes, boxes), :].T[: share - 128]


def downward(sc, ops, mine, other):
    args = (ops, mine, other)
    return call(
        down_kernel,
        sc,
        args,
        [whole(x) for x in args],
        whole(),
        jax.ShapeDtypeStruct((share, boxes), f32),
        12,
        scratch=[
            pltpu.VMEM((tiles * 8 * share, 128), f32),
            pltpu.VMEM((wide, parents), bf16),
            pltpu.VMEM((2 * boxes, 128), f32),
        ],
    )


pitch, step_boxes, unroll = early + 8, 512, 32


def gather_kernel(spots, *refs):
    pieces, o_ref, planes, got = refs[:-3], refs[-3], refs[-2], refs[-1]
    step = pl.program_id(0)
    depth = step_boxes + 8

    @pl.when(step == 0)
    def _():
        at = 0
        for piece in pieces:
            count = piece.shape[0]
            for s in range(tiles):
                planes[pl.ds(s * pitch + at, count), :] = piece[
                    :, s * 128 : (s + 1) * 128
                ].astype(f32)
            at += count
        for s in range(tiles):
            planes[pl.ds(s * pitch + early, 8), :] = jnp.zeros((8, 128), f32)

    def body(i, carry):
        found = [
            planes[pl.ds(spots[step * step_boxes + i * unroll + u], 8, stride=pitch), :]
            for u in range(unroll)
        ]
        for u in range(unroll):
            got[pl.ds(i * unroll + u, 8, stride=depth), :] = found[u]
        return carry

    lax.fori_loop(0, step_boxes // unroll, body, 0)
    for s in range(tiles):
        spot = pl.ds(pl.multiple_of(step * step_boxes, step_boxes), step_boxes)
        o_ref[spot, s * 128 : (s + 1) * 128] = got[pl.ds(s * depth, step_boxes), :].astype(bf16)


def gathered(spots, pieces):
    return call(
        gather_kernel,
        spots,
        tuple(pieces),
        [whole(p) for p in pieces],
        whole(),
        jax.ShapeDtypeStruct((3 * boxes, wide), bf16),
        16,
        grid=(3 * boxes // step_boxes,),
        scratch=[
            pltpu.VMEM((8 * pitch, 128), f32),
            pltpu.VMEM((8 * (step_boxes + 8), 128), f32),
        ],
    )


def far_kernel(start, sc, far, sources, lists, late, late_o, send, keep, result):
    c = sc[0]
    count, most = send.shape[2], result.shape[1]
    late_boxes = jnp.concatenate([late[...], late_o[...]], 0)

    def tile(at, width):
        spot = lax.broadcasted_iota(jnp.int32, (width, 128), 1).astype(f32)
        total = None
        for k in range(3):
            listed = lists[k : k + 1, start + at : start + at + width].astype(f32)
            wanted = jnp.broadcast_to(listed, (128, width)).T
            hot = jnp.concatenate(
                [
                    (wanted == spot + float(base)).astype(f32).astype(bf16)
                    for base in range(0, 2 * chunk, 128)
                ],
                1,
            )
            found = jnp.dot(hot, late_boxes, preferred_element_type=f32)
            found = found + sources[pl.ds(k * boxes + start + at, width), :].astype(f32)
            term = lax.dot_general(
                far[k],
                found.astype(bf16)[:, :rows],
                (((1,), (1,)), ((), ())),
                preferred_element_type=f32,
            )
            total = term if total is None else total + term
        result[:, :width] = total
        lanes = slice(at, at + width)
        for x in (0, 1):
            first = result[pl.ds(share * 2 * x, share), :width]
            second = result[pl.ds(share * (2 * x + 1), share), :width]
            keep[x, :, lanes] = jnp.where(c == 0, first, second)
            send[x, :, lanes] = jnp.where(c == 0, second, first).astype(bf16)

    for at in range(0, count, most):
        tile(at, min(most, count - at))


def far_partial(sc, far, sources, lists, late, late_o, start, count):
    shape = (2, share, count)
    args = (far, sources, lists, late, late_o)
    return call(
        functools.partial(far_kernel, start),
        sc,
        args,
        [whole(x) for x in args],
        [whole(), whole()],
        [jax.ShapeDtypeStruct(shape, bf16), jax.ShapeDtypeStruct(shape, f32)],
        12,
        scratch=[pltpu.VMEM((rows, 256), f32)],
    )


def after(x, *others):
    return lax.optimization_barrier((x, *others))[0]


def local(leaf_density, upward_ops, far_ops, downward_ops, fine_lists, coarse_lists):
    groups = lax.axis_size("space")
    group, rep = lax.axis_index("space"), lax.axis_index("rep")
    l, c = rep >> 1, rep & 1
    no_previous, no_next = group == 0, group == groups - 1
    nowhere = -16384
    base_previous = jnp.where(no_previous, nowhere, 0)
    base_next = jnp.where(no_next, nowhere, 2 * parents)
    sc = jnp.stack(
        [
            c,
            l,
            jnp.where(l == 0, base_previous, base_next),
            jnp.where(l == 0, base_next, base_previous),
        ]
    ).astype(jnp.int32)
    hop = functools.partial(lax.ppermute, axis_name=both, perm=one_hop(groups))
    zswap = functools.partial(lax.ppermute, axis_name=both, perm=across(groups, 2))
    cswap = functools.partial(lax.ppermute, axis_name=both, perm=across(groups, 1))

    def at(i):
        return jnp.reshape(i, (1,)).astype(jnp.int32)

    up_ops = jnp.transpose(upward_ops, (1, 0, 2)).reshape(8 * share, rows)
    down_ops = jnp.transpose(downward_ops, (1, 0, 2)).reshape(8 * share, rows)

    which, side, offset = fine_lists >> 10, (fine_lists >> 9) & 1, fine_lists & (half - 1)
    outside = ((which == 0) & no_previous) | ((which == 2) & no_next)
    direct = (which == 0) == (l == 0)
    theirs = (side != c).astype(jnp.int32)
    is_late = (which != 1) & ~direct & (offset >= half - chunk)
    spots = jnp.where(
        which == 1,
        theirs * half + offset,
        jnp.where(
            direct,
            2 * half + theirs * half + offset,
            4 * half + theirs * (half - chunk) + offset,
        ),
    )
    spots = jnp.where(outside | is_late, early, spots).reshape(-1)
    late_lists = jnp.where(is_late & ~outside, theirs * chunk + offset - (half - chunk), -1)

    head = turned(leaf_density, at(c * half), [chunk])[0]
    rest = jnp.stack([c * half + chunk, (1 - c) * half]).astype(jnp.int32)
    tail, other = turned(leaf_density, after(rest, head), [half - chunk, half])
    up = parent_rows(after(sc, spots, late_lists), up_ops, [head, tail], other)
    own = joined(sc, up, zswap(up))
    ca = hop(own)
    own_o = cswap(own)
    mine = [head, after(tail, up)]
    a = [hop(m) for m in mine]
    early_a = after(a[0], own)
    second = after(a[1], early_a, own_o)
    b = [zswap(early_a), zswap(second)]
    a_o = [cswap(early_a), cswap(after(second, ca))]
    cb, ca_o = zswap(ca), cswap(ca)
    b_o = [cswap(b[0])]
    picked = gathered(spots, [*mine, other, *a, *a_o, b[0], b_o[0]])
    b_o.append(cswap(after(b[1], picked)))
    cb_o = cswap(cb)

    def summed(send, keep):
        shape = (share, send.shape[2])
        here, away = small(split_kernel, sc, (keep, cswap(send)), [(shape, f32), (shape, bf16)])
        return here, zswap(away), away

    late = (b[1], b_o[1])
    send, keep = far_partial(sc, far_ops, picked, late_lists, *late, 0, ahead)
    left = summed(after(send, cb_o, ca_o), keep)
    send, keep = coarse_partial(
        after(sc, send), coarse_lists, far_ops, own, ca, cb, own_o, ca_o, cb_o
    )
    shape = (wide // 2, parents)
    part, part_sent = small(
        add_kernel, after(sc, left[2]), (keep, cswap(send)), [(shape, f32), (shape, bf16)]
    )
    send, keep = far_partial(
        after(sc, part), far_ops, picked, late_lists, *late, ahead, boxes - ahead
    )
    part_got = zswap(part_sent)
    right = summed(after(send, left[1], part_got), keep)
    check = small(add_kernel, sc, (part, part_got), [(shape, bf16)])[0]
    check_o = cswap(check)
    spread = downward(after(sc, right[2]), down_ops, check, check_o)
    return small(last_kernel, sc, (spread, *left[:2], *right[:2]), [((share, boxes), bf16)])[0]


def solution(mesh):
    return jax.shard_map(
        local,
        mesh=mesh,
        in_specs=(
            P(None, "space"),
            P(None, "rep", None),
            P("rep", None, None),
            P(None, "rep", None),
            P("rep", "space"),
            P("rep", "space"),
        ),
        out_specs=P("rep", "space"),
        check_vma=False,
    )
```

```python
import functools

import jax
import jax.numpy as jnp
from jax import lax
from jax.experimental import pallas as pl
from jax.experimental.pallas import tpu as pltpu
from jax.sharding import PartitionSpec as P

bf16, f32 = jnp.bfloat16, jnp.float32
both = ("space", "rep")
coarse_scale = 0.5
rows, wide, tiles = 888, 896, 7
boxes, half = 1024, 512
parents = 128
share = 222
chunks = 2
chunk = half // chunks
early = 6 * half - 2 * chunk
ahead = 640


def one_hop(groups):
    up = [(4 * s + 2 + c, 4 * (s + 1) + c) for s in range(groups - 1) for c in (0, 1)]
    up += [(0, 1), (4 * groups - 2, 4 * groups - 1)]
    return up + [(j, i) for i, j in up]


def across(groups, flip):
    return [(4 * s + r, 4 * s + (r ^ flip)) for s in range(groups) for r in range(4)]


def call(kernel, scalars, args, in_specs, out_specs, out_shape, limit, grid=(1,), scratch=()):
    return pl.pallas_call(
        kernel,
        grid_spec=pltpu.PrefetchScalarGridSpec(
            num_scalar_prefetch=1,
            grid=grid,
            in_specs=in_specs,
            out_specs=out_specs,
            scratch_shapes=scratch,
        ),
        out_shape=out_shape,
        compiler_params=pltpu.CompilerParams(vmem_limit_bytes=limit << 20),
        cost_estimate=pl.CostEstimate(flops=0, bytes_accessed=0, transcendentals=0),
    )(scalars, *args)


def whole(a=None):
    return pl.BlockSpec(memory_space=pltpu.VMEM)


def turn_kernel(firsts, x_ref, *outs):
    for n, o_ref in enumerate(outs):
        for i in range(o_ref.shape[0] // 128):
            part = x_ref[:, pl.ds(pl.multiple_of(firsts[n] + i * 128, 128), 128)].astype(f32)
            tall = jnp.concatenate([part, jnp.zeros((wide - rows, 128), f32)], 0)
            o_ref[pl.ds(i * 128, 128), :] = tall.T.astype(bf16)


def turned(x, firsts, counts):
    shapes = [jax.ShapeDtypeStruct((n, wide), bf16) for n in counts]
    return call(turn_kernel, firsts, (x,), [whole()], [whole() for _ in counts], shapes, 8)


def small(kernel, sc, args, shapes, limit=6):
    shapes = [jax.ShapeDtypeStruct(*s) for s in shapes]
    return call(kernel, sc, args, [whole() for _ in args], [whole() for _ in shapes], shapes, limit)


def join_kernel(sc, *refs):
    at = 0
    for part in refs[:-1]:
        refs[-1][:, at : at + part.shape[1]] = part[...]
        at += part.shape[1]


def joined(sc, *parts):
    width = sum(p.shape[1] for p in parts)
    return small(join_kernel, sc, parts, [((parts[0].shape[0], width), bf16)])[0]


def split_kernel(sc, keep, got, here, away):
    l = sc[1]
    here[...] = keep[l] + got[l].astype(f32)
    away[...] = (keep[1 - l] + got[1 - l].astype(f32)).astype(bf16)


def add_kernel(sc, one, two, *outs):
    total = one[...] + two[...].astype(f32)
    for o_ref in outs:
        o_ref[...] = total.astype(o_ref.dtype)


def last_kernel(sc, spread, *refs):
    o_ref, at = refs[-1], 0
    for here, there in zip(refs[:-1:2], refs[1:-1:2]):
        lanes = slice(at, at + here.shape[1])
        o_ref[:, lanes] = (here[...] + there[...].astype(f32) + spread[:, lanes]).astype(bf16)
        at += here.shape[1]


def to_planes(src, dst, height):
    for s in range(tiles - 1):
        dst[pl.ds(s * height, height), :] = src[:, s * 128 : (s + 1) * 128].astype(f32)
    last = src[:, (tiles - 1) * 128 :].astype(f32)
    if last.shape[1] < 128:
        last = jnp.concatenate([last, jnp.zeros((height, 128 - last.shape[1]), f32)], 1)
    dst[pl.ds((tiles - 1) * height, height), :] = last


def every_eighth(planes, height, child, count):
    parts = [planes[pl.ds(s * height + child, count, stride=8), :] for s in range(tiles)]
    return jnp.concatenate(parts, 1).astype(bf16)


def up_kernel(sc, ops, other, *refs):
    mine, o_ref, op_planes, box_planes = refs[:-3], refs[-3], refs[-2], refs[-1]
    to_planes(ops, op_planes, 8 * share)
    for s in range(tiles):
        lanes = slice(s * 128, (s + 1) * 128)
        for i, part in enumerate(mine):
            at = pl.multiple_of(s * boxes + sc[0] * half + i * chunk, chunk)
            box_planes[pl.ds(at, chunk), :] = part[:, lanes].astype(f32)
        at = pl.multiple_of(s * boxes + (1 - sc[0]) * half, half)
        box_planes[pl.ds(at, half), :] = other[:, lanes].astype(f32)
    total = None
    for child in range(8):
        left = every_eighth(op_planes, 8 * share, child, share)
        right = every_eighth(box_planes, boxes, child, parents)
        term = lax.dot_general(left, right, (((1,), (1,)), ((), ())), preferred_element_type=f32)
        total = term if total is None else total + term
    o_ref[...] = total.astype(bf16)


def parent_rows(sc, ops, mine, other):
    args = (ops, other, *mine)
    return call(
        up_kernel,
        sc,
        args,
        [whole(a) for a in args],
        whole(),
        jax.ShapeDtypeStruct((share, parents), bf16),
        14,
        scratch=[
            pltpu.VMEM((tiles * 8 * share, 128), f32),
            pltpu.VMEM((tiles * boxes, 128), f32),
        ],
    )


def coarse_kernel(sc, lists, far, own, a, b, own_o, a_o, b_o, send, keep, picked, result):
    c, l = sc[0], sc[1]
    wanted = jnp.concatenate([lists[k : k + 1, :] for k in range(3)], 1)
    count = wanted.shape[1]
    spot = lax.broadcasted_iota(jnp.int32, (parents, count), 0)
    hot = jnp.concatenate(
        [
            (spot == wanted - base).astype(f32).astype(bf16)
            for base in (parents, sc[2], sc[3])
        ],
        0,
    )

    def pick(*parts):
        return jnp.dot(jnp.concatenate(parts, 1), hot, preferred_element_type=f32)

    lo, hi = slice(0, parents), slice(parents, 2 * parents)
    found = (
        (pick(own[:, lo], a[:, hi], b[:, lo]), pick(own[:, hi], a[:, lo], b[:, hi])),
        (pick(own_o[:, lo], a_o[:, hi], b_o[:, lo]), pick(own_o[:, hi], a_o[:, lo], b_o[:, hi])),
    )
    for j in range(4):
        x, y = j // 2, j % 2
        mine = jnp.where(l == x, found[0][0], found[0][1])
        theirs = jnp.where(l == x, found[1][0], found[1][1])
        picked[pl.ds(share * j, share), :] = jnp.where(c == y, mine, theirs)
    sources = picked[...].astype(bf16)
    total = None
    for k in range(3):
        term = jnp.dot(
            far[k], sources[:, k * parents : (k + 1) * parents], preferred_element_type=f32
        )
        total = term if total is None else total + term
    result[pl.ds(0, rows), :] = total * coarse_scale
    result[pl.ds(rows, wide - rows), :] = jnp.zeros((wide - rows, parents), f32)
    part = wide // 2
    keep[...] = result[pl.ds(pl.multiple_of(c * part, part), part), :]
    send[...] = result[pl.ds(pl.multiple_of((1 - c) * part, part), part), :].astype(bf16)


def coarse_partial(sc, lists, far, own, a, b, own_o, a_o, b_o):
    args = (lists, far, own, a, b, own_o, a_o, b_o)
    shape = (wide // 2, parents)
    return call(
        coarse_kernel,
        sc,
        args,
        [whole(x) for x in args],
        [whole(), whole()],
        [jax.ShapeDtypeStruct(shape, bf16), jax.ShapeDtypeStruct(shape, f32)],
        8,
        scratch=[pltpu.VMEM((rows, 3 * parents), f32), pltpu.VMEM((wide, parents), f32)],
    )


def down_kernel(sc, ops, mine, other, o_ref, op_planes, check, turned_rows):
    c, part = sc[0], wide // 2
    to_planes(ops, op_planes, 8 * share)
    check[pl.ds(pl.multiple_of(c * part, part), part), :] = mine[...]
    check[pl.ds(pl.multiple_of((1 - c) * part, part), part), :] = other[...]
    whole_check = check[...]
    for child in range(8):
        left = every_eighth(op_planes, 8 * share, child, share)
        z = jnp.dot(left, whole_check, preferred_element_type=f32)
        z = jnp.concatenate([z, jnp.zeros((256 - share, parents), f32)], 0).T
        for t in (0, 1):
            turned_rows[pl.ds(t * boxes + child, parents, stride=8), :] = z[
                :, t * 128 : (t + 1) * 128
            ]
    o_ref[pl.ds(0, 128), :] = turned_rows[pl.ds(0, boxes), :].T
    o_ref[pl.ds(128, share - 128), :] = turned_rows[pl.ds(boxes, boxes), :].T[: share - 128]


def downward(sc, ops, mine, other):
    args = (ops, mine, other)
    return call(
        down_kernel,
        sc,
        args,
        [whole(x) for x in args],
        whole(),
        jax.ShapeDtypeStruct((share, boxes), f32),
        12,
        scratch=[
            pltpu.VMEM((tiles * 8 * share, 128), f32),
            pltpu.VMEM((wide, parents), bf16),
            pltpu.VMEM((2 * boxes, 128), f32),
        ],
    )


pitch, step_boxes, unroll = early + 8, 512, 32


def gather_kernel(spots, *refs):
    pieces, o_ref, planes, got = refs[:-3], refs[-3], refs[-2], refs[-1]
    step = pl.program_id(0)
    depth = step_boxes + 8

    @pl.when(step == 0)
    def _():
        at = 0
        for piece in pieces:
            count = piece.shape[0]
            for s in range(tiles):
                planes[pl.ds(s * pitch + at, count), :] = piece[
                    :, s * 128 : (s + 1) * 128
                ].astype(f32)
            at += count
        for s in range(tiles):
            planes[pl.ds(s * pitch + early, 8), :] = jnp.zeros((8, 128), f32)

    def body(i, carry):
        found = [
            planes[pl.ds(spots[step * step_boxes + i * unroll + u], 8, stride=pitch), :]
            for u in range(unroll)
        ]
        for u in range(unroll):
            got[pl.ds(i * unroll + u, 8, stride=depth), :] = found[u]
        return carry

    lax.fori_loop(0, step_boxes // unroll, body, 0)
    for s in range(tiles):
        spot = pl.ds(pl.multiple_of(step * step_boxes, step_boxes), step_boxes)
        o_ref[spot, s * 128 : (s + 1) * 128] = got[pl.ds(s * depth, step_boxes), :].astype(bf16)


def gathered(spots, pieces):
    return call(
        gather_kernel,
        spots,
        tuple(pieces),
        [whole(p) for p in pieces],
        whole(),
        jax.ShapeDtypeStruct((3 * boxes, wide), bf16),
        16,
        grid=(3 * boxes // step_boxes,),
        scratch=[
            pltpu.VMEM((8 * pitch, 128), f32),
            pltpu.VMEM((8 * (step_boxes + 8), 128), f32),
        ],
    )


def far_kernel(start, sc, far, sources, lists, late, late_o, send, keep, result):
    c = sc[0]
    count, most = send.shape[2], result.shape[1]
    late_boxes = jnp.concatenate([late[...], late_o[...]], 0)

    def tile(at, width):
        spot = lax.broadcasted_iota(jnp.int32, (width, 128), 1).astype(f32)
        total = None
        for k in range(3):
            listed = lists[k : k + 1, start + at : start + at + width].astype(f32)
            wanted = jnp.broadcast_to(listed, (128, width)).T
            hot = jnp.concatenate(
                [
                    (wanted == spot + float(base)).astype(f32).astype(bf16)
                    for base in range(0, 2 * chunk, 128)
                ],
                1,
            )
            found = jnp.dot(hot, late_boxes, preferred_element_type=f32)
            found = found + sources[pl.ds(k * boxes + start + at, width), :].astype(f32)
            term = lax.dot_general(
                far[k],
                found.astype(bf16)[:, :rows],
                (((1,), (1,)), ((), ())),
                preferred_element_type=f32,
            )
            total = term if total is None else total + term
        result[:, :width] = total
        lanes = slice(at, at + width)
        for x in (0, 1):
            first = result[pl.ds(share * 2 * x, share), :width]
            second = result[pl.ds(share * (2 * x + 1), share), :width]
            keep[x, :, lanes] = jnp.where(c == 0, first, second)
            send[x, :, lanes] = jnp.where(c == 0, second, first).astype(bf16)

    for at in range(0, count, most):
        tile(at, min(most, count - at))


def far_partial(sc, far, sources, lists, late, late_o, start, count):
    shape = (2, share, count)
    args = (far, sources, lists, late, late_o)
    return call(
        functools.partial(far_kernel, start),
        sc,
        args,
        [whole(x) for x in args],
        [whole(), whole()],
        [jax.ShapeDtypeStruct(shape, bf16), jax.ShapeDtypeStruct(shape, f32)],
        12,
        scratch=[pltpu.VMEM((rows, 256), f32)],
    )


def after(x, *others):
    return lax.optimization_barrier((x, *others))[0]


def local(leaf_density, upward_ops, far_ops, downward_ops, fine_lists, coarse_lists):
    groups = lax.axis_size("space")
    group, rep = lax.axis_index("space"), lax.axis_index("rep")
    l, c = rep >> 1, rep & 1
    no_previous, no_next = group == 0, group == groups - 1
    nowhere = -16384
    base_previous = jnp.where(no_previous, nowhere, 0)
    base_next = jnp.where(no_next, nowhere, 2 * parents)
    sc = jnp.stack(
        [
            c,
            l,
            jnp.where(l == 0, base_previous, base_next),
            jnp.where(l == 0, base_next, base_previous),
        ]
    ).astype(jnp.int32)
    hop = functools.partial(lax.ppermute, axis_name=both, perm=one_hop(groups))
    zswap = functools.partial(lax.ppermute, axis_name=both, perm=across(groups, 2))
    cswap = functools.partial(lax.ppermute, axis_name=both, perm=across(groups, 1))

    def at(i):
        return jnp.reshape(i, (1,)).astype(jnp.int32)

    up_ops = jnp.transpose(upward_ops, (1, 0, 2)).reshape(8 * share, rows)
    down_ops = jnp.transpose(downward_ops, (1, 0, 2)).reshape(8 * share, rows)

    which, side, offset = fine_lists >> 10, (fine_lists >> 9) & 1, fine_lists & (half - 1)
    outside = ((which == 0) & no_previous) | ((which == 2) & no_next)
    direct = (which == 0) == (l == 0)
    theirs = (side != c).astype(jnp.int32)
    is_late = (which != 1) & ~direct & (offset >= half - chunk)
    spots = jnp.where(
        which == 1,
        theirs * half + offset,
        jnp.where(
            direct,
            2 * half + theirs * half + offset,
            4 * half + theirs * (half - chunk) + offset,
        ),
    )
    spots = jnp.where(outside | is_late, early, spots).reshape(-1)
    late_lists = jnp.where(is_late & ~outside, theirs * chunk + offset - (half - chunk), -1)

    head = turned(leaf_density, at(c * half), [chunk])[0]
    rest = jnp.stack([c * half + chunk, (1 - c) * half]).astype(jnp.int32)
    tail, other = turned(leaf_density, after(rest, head), [half - chunk, half])
    up = parent_rows(after(sc, spots, late_lists), up_ops, [head, tail], other)
    own = joined(sc, up, zswap(up))
    ca = hop(own)
    own_o = cswap(own)
    mine = [head, after(tail, up)]
    a = [hop(m) for m in mine]
    early_a = after(a[0], own)
    second = after(a[1], early_a, own_o)
    b = [zswap(early_a), zswap(second)]
    a_o = [cswap(early_a), cswap(after(second, ca))]
    cb, ca_o = zswap(ca), cswap(ca)
    b_o = [cswap(b[0])]
    picked = gathered(spots, [*mine, other, *a, *a_o, b[0], b_o[0]])
    b_o.append(cswap(after(b[1], picked, cb)))
    cb_o = cswap(cb)

    def summed(send, keep):
        shape = (share, send.shape[2])
        here, away = small(split_kernel, sc, (keep, cswap(send)), [(shape, f32), (shape, bf16)])
        return here, zswap(away), away

    late = (b[1], b_o[1])
    send, keep = far_partial(sc, far_ops, picked, late_lists, *late, 0, ahead)
    left = summed(after(send, cb_o, ca_o), keep)
    send, keep = coarse_partial(
        after(sc, send), coarse_lists, far_ops, own, ca, cb, own_o, ca_o, cb_o
    )
    shape = (wide // 2, parents)
    part, part_sent = small(
        add_kernel, after(sc, left[2]), (keep, cswap(send)), [(shape, f32), (shape, bf16)]
    )
    send, keep = far_partial(
        after(sc, part), far_ops, picked, late_lists, *late, ahead, boxes - ahead
    )
    part_got = zswap(part_sent)
    right = summed(after(send, left[1], part_got), keep)
    check = small(add_kernel, sc, (part, part_got), [(shape, bf16)])[0]
    check_o = cswap(check)
    spread = downward(after(sc, right[2]), down_ops, check, check_o)
    return small(last_kernel, sc, (spread, *left[:2], *right[:2]), [((share, boxes), bf16)])[0]


def solution(mesh):
    return jax.shard_map(
        local,
        mesh=mesh,
        in_specs=(
            P(None, "space"),
            P(None, "rep", None),
            P("rep", None, None),
            P(None, "rep", None),
            P("rep", "space"),
            P("rep", "space"),
        ),
        out_specs=P("rep", "space"),
        check_vma=False,
    )
```
